256 devices in a mesh: lvl: 4 (over y), cell: 64 (over x, z, core).
Axes of the slice: x: 4, y: 4, z: 8, core: 2. Of those that a mesh axis runs over, the one named last changes fastest.
Arguments:
- rhs: float32 [16, 1024, 1024], P('lvl', 'cell'), may hold values from -6 to 6
- adjoint_owned: float32 [16, 1024, 1024], P('lvl', 'cell'), may hold values from -6 to 6
- owner_of: int32 [16, 1024], P('lvl', 'cell'), may hold values from 0 to 16383, as said below
- columns: int32 [16, 1024, 3], P('lvl', 'cell'), may hold values from 0 to 1023, as said below
- lower: float32 [16, 1024, 3, 4096], P('lvl', 'cell'), may hold values from -0.4375 to 0.4375
- dinv: float32 [16, 1024, 4096], P('lvl', 'cell'), may hold values from -0.3 to 1, as said below
Outputs:
- solved: float32 [16, 1024, 1024], P('lvl', 'cell')
- adjoint: float32 [16, 1024, 1024], P('lvl', 'cell')
The draws below stay inside these ranges and needn't reach their ends.
Inputs may be any that keep to these rules, and one draw needn't show every extreme that they name: `columns`: entry k of block row q of level l names a row of level l - 1 whose position differs from q by at most 8 cyclically over 1024 rows; the 3 entries of a row differ. `owner_of`: A permutation that keeps each section of 4 consecutive levels within itself. Numbering a device's owner positions m = (level mod 4) * 16 + (row mod 16), the block row q of level order sits at an owner position whose m, modulo the number of devices along cell, equals q // 16. `dinv`: diagonal entries of each block between 0.6 and 1.
All inputs are finite; a program needn't handle non-finite values.
Results may differ from the reference program's by a relative error of at most 0.00011.
Values sent between devices are 32-bit elements; how exact they have to be, the bound alone decides.
No kernel may reach another device: no remote copies, remote signals or barrier semaphores. Data moves between devices by JAX's collectives and lax.ppermute only.
A program may use at most 192 MiB of HBM per device.

```python
import jax
import jax.numpy as jnp
from jax import lax

B = 64
NV = 16
K = 3
W = 8
LPS = 4
RL = 16
NLEV = 16
LR = 1024


def draw_dinv(key, part):
    key = jax.random.fold_in(key, 11)
    key_diag, key_off = jax.random.split(key)
    shape = (NLEV, LR, B * B)
    identity = jnp.eye(B, dtype=jnp.float32).reshape(B * B)
    diagonal = jax.random.uniform(key_diag, shape, jnp.float32, 0.6, 1.0)
    off_part = jnp.clip(0.05 * jax.random.normal(key_off, shape, jnp.float32), -0.3, 0.3)
    return jnp.where(identity[None, None, :] > 0.5, diagonal, off_part)


def draw_columns(key, part):
    key = jax.random.fold_in(key, 12)
    key_list = jax.random.split(key, NLEV * LR)
    offsets = jax.vmap(lambda single: jax.random.permutation(single, 2 * W + 1)[:K])(key_list)
    offsets = offsets.astype(jnp.int32).reshape(NLEV, LR, K) - W
    row_ids = jnp.arange(LR, dtype=jnp.int32)[None, :, None]
    return ((row_ids + offsets) % LR).astype(jnp.int32)


def draw_owner_of(key, part):
    key = jax.random.fold_in(key, 13)
    cell_count = LR // RL
    section_count = NLEV // LPS
    block_rows = LPS * RL
    per_peer = block_rows // cell_count
    key_list = jax.random.split(key, section_count * cell_count)
    shuffles = jax.vmap(lambda single: jax.random.permutation(single, block_rows))(key_list).astype(jnp.int32)
    level_ids = jnp.arange(NLEV, dtype=jnp.int32)[:, None]
    row_ids = jnp.arange(LR, dtype=jnp.int32)[None, :]
    section = level_ids // LPS
    target_cell = row_ids // RL
    local_row = level_ids % LPS * RL + row_ids % RL
    picked = shuffles[section * cell_count + target_cell, local_row]
    source_cell = picked // per_peer
    owner_local = picked % per_peer * cell_count + target_cell
    owner_level = section * LPS + owner_local // RL
    owner_row = source_cell * RL + owner_local % RL
    return (owner_level * LR + owner_row).astype(jnp.int32)


def levels(stream_key, extent, pieces, least, high):
    factor_of, own = 1.0, jax.random.fold_in(stream_key, 6)
    for position, parts in pieces:
        steps = jnp.exp(jax.random.uniform(jax.random.fold_in(own, position), (parts,), jnp.float32, least / len(pieces), high / len(pieces)))
        factor_of = factor_of * jnp.repeat(steps, extent[position] // parts).reshape([-1 if axis == position else 1 for axis in range(len(extent))])
    return factor_of


def scatter_about(stream_key, extent, scale, limit, cuts=(), held_as=jnp.bfloat16):
    drawn = scale * jax.random.normal(stream_key, extent, jnp.float32)
    if cuts:
        drawn = drawn * levels(stream_key, extent, cuts, -0.22, 0.18)
    return jnp.clip(drawn, -limit, limit).astype(held_as)


def setup_inputs(seed: int = 0) -> dict:
    seeds = jax.random.split(jax.random.key(seed), 7)
    rhs = scatter_about(seeds[0], (NLEV, LR, B * NV), 1.0, 6.0, ((0, 4), (1, 64)), jnp.float32)
    adjoint_owned = scatter_about(seeds[1], (NLEV, LR, B * NV), 1.0, 6.0, ((0, 4), (1, 64)), jnp.float32)
    owner_of = draw_owner_of(jax.random.fold_in(seeds[6], 71), 0)
    columns = draw_columns(jax.random.fold_in(seeds[6], 71), 0)
    lower = scatter_about(seeds[4], (NLEV, LR, K, B * B), (K * B) ** -0.5, 0.4375, ((0, 4), (1, 64)), jnp.float32)
    dinv = draw_dinv(jax.random.fold_in(seeds[6], 71), 0)
    return dict(rhs=rhs, adjoint_owned=adjoint_owned, owner_of=owner_of, columns=columns, lower=lower, dinv=dinv)


def reference(rhs, adjoint_owned, owner_of, columns, lower, dinv):
    highest = lax.Precision.HIGHEST
    level_count, span_rows, feat_width = rhs.shape
    vec_count = feat_width // B
    adjoint_level = jnp.take(adjoint_owned.reshape(level_count * span_rows, feat_width), owner_of.reshape(-1), axis=0).reshape(level_count, span_rows, feat_width)
    zero_rows = jnp.zeros((span_rows, feat_width), jnp.float32)

    def forward_step(previous, inputs):
        source, targets, blocks, inverse = inputs
        gathered = jnp.take(previous, targets.reshape(-1), axis=0).reshape(span_rows, K, B, vec_count)
        coupled = jnp.einsum("rkab,rkbv->rav", blocks.reshape(span_rows, K, B, B), gathered, precision=highest)
        remain = source.reshape(span_rows, B, vec_count) - coupled
        result = jnp.einsum("rab,rbv->rav", inverse.reshape(span_rows, B, B), remain, precision=highest).reshape(span_rows, feat_width)
        return result, result

    unused, solved_all = lax.scan(forward_step, zero_rows, (rhs, columns, lower, dinv))

    def backward_step(pending, inputs):
        source, targets, blocks, inverse = inputs
        remain = source.reshape(span_rows, B, vec_count) - pending.reshape(span_rows, B, vec_count)
        result = jnp.einsum("rba,rbv->rav", inverse.reshape(span_rows, B, B), remain, precision=highest)
        spread = jnp.einsum("rkba,rbv->rkav", blocks.reshape(span_rows, K, B, B), result, precision=highest).reshape(span_rows * K, feat_width)
        lower_terms = jnp.zeros((span_rows, feat_width), jnp.float32).at[targets.reshape(-1)].add(spread)
        return lower_terms, result.reshape(span_rows, feat_width)

    unused, adjoint_all = lax.scan(backward_step, zero_rows, (adjoint_level, columns, lower, dinv), reverse=True)
    return solved_all, adjoint_all
```

```python
from functools import partial

import jax
import jax.numpy as jnp
from jax import lax
from jax.experimental import pallas as pl
from jax.experimental.pallas import tpu as pltpu
from jax.sharding import PartitionSpec as P

B = 64
NV = 16
K = 3
W = 8
LV = 4
RL = 16
ROWS = LV * RL
EXT = RL + 2 * W
VMEM = pltpu.VMEM
SMEM = pltpu.SMEM
F32 = jnp.float32
BF16 = jnp.bfloat16
MIB = 1 << 20


def in_vmem(x):
    return pltpu.with_memory_space_constraint(x, VMEM)


def in_smem(x):
    return pltpu.with_memory_space_constraint(x, SMEM)


def split(x):
    hi = x.astype(BF16)
    lo = (x - hi.astype(F32)).astype(BF16)
    return hi, lo


def nn(a, b):
    return jnp.dot(a, b, preferred_element_type=F32)


def nt(a, b):
    return lax.dot_general(a, b, (((1,), (1,)), ((), ())), preferred_element_type=F32)


def low_half(shape):
    return lax.broadcasted_iota(jnp.int32, shape, len(shape) - 1) % 128 < B


def other_half(x):
    return pltpu.roll(x, B, axis=x.ndim - 1)


def spread_matrix():
    row = lax.broadcasted_iota(jnp.int32, (B * NV, 128), 0) // NV
    col = lax.broadcasted_iota(jnp.int32, (B * NV, 128), 1) % B
    return jnp.where(row == col, 1.0, 0.0).astype(BF16)


def own_lane(rows):
    lane = lax.broadcasted_iota(jnp.int32, (rows, 128), 1) % NV
    vec = lax.broadcasted_iota(jnp.int32, (rows, 128), 0) % NV
    return lane == vec


def state_of_rows(load, count, spread):
    mask = own_lane(NV)
    highs, lows = [], []
    for row in range(count):
        chunks_hi, chunks_lo = [], []
        for chunk in range(B * NV // 128):
            value = jnp.broadcast_to(load(row, chunk), (NV, 128))
            value = jnp.where(mask, value, 0.0)
            hi, lo = split(value)
            chunks_hi.append(hi)
            chunks_lo.append(lo)
        highs.append(jnp.concatenate(chunks_hi, axis=1))
        lows.append(jnp.concatenate(chunks_lo, axis=1))
    out = nn(jnp.concatenate(highs, axis=0), spread) + nn(jnp.concatenate(lows, axis=0), spread)
    return out.reshape(count, NV, 128)


def prep_kernel(index_ref, rhs_ref, lower_hbm, dinv_hbm, w_ref, r_ref, s_ref, low, din, tiles, both, sems):
    def copies(level):
        return (
            pltpu.make_async_copy(lower_hbm.at[level], low.at[level], sems.at[0, level]),
            pltpu.make_async_copy(dinv_hbm.at[level], din.at[level], sems.at[1, level]),
        )

    for level in range(LV):
        for copy in copies(level):
            copy.start()

    def copy_index(i, carry):
        s_ref[i] = index_ref[i]
        return carry

    lax.fori_loop(0, index_ref.shape[0], copy_index, 0)
    spread = spread_matrix()

    def rhs_part(i, carry):
        level, half = i // 2, i % 2
        block = rhs_ref[level, pl.ds(pl.multiple_of(half * 8, 8), 8), :]
        for part in range(2):

            def load(row, chunk):
                return block[part * 4 + row:part * 4 + row + 1, chunk * 128:(chunk + 1) * 128]

            r_ref[pl.ds(i * 8 + part * 4, 4)] = state_of_rows(load, 4, spread)
        return carry

    lax.fori_loop(0, LV * 2, rhs_part, 0)
    left = low_half((B // 2, 128))
    left_wide = low_half((B, 128))

    for level in range(LV):
        for copy in copies(level):
            copy.wait()

        def half_level(half, carry):
            start = pl.multiple_of(half * 8, 8)
            for k in range(K + 1):
                for chunk in range(B * B // 128):
                    lanes = pl.ds(chunk * 128, 128)
                    if k < K:
                        value = low[level, k, pl.ds(start, 8), lanes]
                    else:
                        value = din[level, pl.ds(start, 8), lanes]
                    tiles[k, pl.ds(chunk * 8, 8), :] = value
            for row in range(8):
                part = [tiles[k, pl.ds(row, B // 2, stride=8), :] for k in range(K + 1)]
                turned = [other_half(p) for p in part]
                slot = row % 2
                both[slot, 0, pl.ds(0, B // 2, stride=2), :] = jnp.where(left, part[0], turned[1])
                both[slot, 0, pl.ds(1, B // 2, stride=2), :] = jnp.where(left, turned[0], part[1])
                both[slot, 1, pl.ds(0, B // 2, stride=2), :] = jnp.where(left, part[2], turned[3])
                both[slot, 1, pl.ds(1, B // 2, stride=2), :] = jnp.where(left, turned[2], part[3])
                first, second = both[slot, 0], both[slot, 1]
                diag = other_half(second)[:, :B]
                diag_hi, diag_lo = split(diag)
                right_hi, right_lo = split(jnp.concatenate([first, second], axis=1))
                top = nn(jnp.concatenate([diag_hi, diag_lo], axis=0), right_hi)
                product = top[:B] + top[B:] + nn(diag_hi, right_lo)
                tail = jnp.where(left_wide, product[:, 128:], second)
                hi, lo = split(jnp.concatenate([product[:, :128], tail], axis=1))
                w_ref[level * RL + start + row] = jnp.concatenate([hi, lo], axis=0)
            return carry

        lax.fori_loop(0, 2, half_level, 0)


def adjoint_kernel(index_ref, relayed_ref, a_ref):
    spread = spread_matrix()

    def part(i, carry):
        def load(row, chunk):
            return relayed_ref[index_ref[K * ROWS + i * 4 + row], pl.ds(chunk, 1), :]

        a_ref[pl.ds(i * 4, 4)] = state_of_rows(load, 4, spread)
        return carry

    lax.fori_loop(0, ROWS // 4, part, 0)


def pack(x):
    half = x.shape[0] // 2
    return jnp.where(low_half((half, NV, 128)), x[:half], x[half:])


def unpack(x):
    turned = other_half(x)
    left = low_half(x.shape)
    return jnp.concatenate([jnp.where(left, x, turned), jnp.where(left, turned, x)], axis=0)


FLAGS = (K + 1) * ROWS


def step_kernel(step, cross, turn, s_ref, w_ref, r_ref, a_ref, own_ref, left_ref, right_ref,
                sol_in, adj_in, sol_ref, adj_ref, out_ref, outl_ref, outr_ref, ext, acc0, acc1, acc2):
    del sol_in, adj_in
    section = s_ref[FLAGS]
    even = s_ref[FLAGS + 1] == 0
    half = low_half((NV, 128))

    def incoming(do):
        if own_ref is None:
            return
        if not cross:
            do(left_ref, right_ref)
        else:
            pl.when(even)(lambda: do(right_ref, left_ref))
            pl.when(jnp.logical_not(even))(lambda: do(left_ref, right_ref))

    def outgoing(to_left, to_right):
        if not turn:
            outl_ref[...] = to_left
            outr_ref[...] = to_right
        else:
            @pl.when(even)
            def _():
                outl_ref[...] = to_right
                outr_ref[...] = to_left

            @pl.when(jnp.logical_not(even))
            def _():
                outl_ref[...] = to_left
                outr_ref[...] = to_right

    rnd, t = divmod(step, LV)

    @pl.when(section == rnd)
    def _():
        level = t
        first = step == 0
        if not first:
            ext[pl.ds(W, RL)] = unpack(own_ref[...])

            def fill(from_left, from_right):
                ext[pl.ds(0, W)] = unpack(from_left[...])
                ext[pl.ds(W + RL, W)] = unpack(from_right[...])

            incoming(fill)
        results = []
        for row in range(RL):
            flat = level * RL + row
            source = r_ref[flat]
            if first:
                lhs = jnp.concatenate([jnp.zeros_like(source), jnp.where(half, 0.0, -source)], axis=1)
            else:
                x0, x1, x2 = [ext[s_ref[flat * K + k]] for k in range(K)]
                lhs = jnp.concatenate([jnp.where(half, x0, x1), jnp.where(half, x2, -source)], axis=1)
            hi, lo = split(lhs)
            out = nt(jnp.concatenate([hi, lo], axis=0), w_ref[flat])
            out = out[:NV] + out[NV:]
            out = -(out + other_half(out))
            sol_ref[flat] = out
            results.append(out)
        x = jnp.stack(results)
        out_ref[...] = pack(x)
        outgoing(pack(x[:W]), pack(x[W:]))

    @pl.when(section == LV - 1 - rnd)
    def _():
        level = LV - 1 - t
        first = step == 0
        if not first:
            ext[pl.ds(0, RL)] = unpack(own_ref[...])

            def add(from_left, from_right):
                ext[pl.ds(0, W)] += unpack(from_left[...])
                ext[pl.ds(W, W)] += unpack(from_right[...])

            incoming(add)
        zeros = jnp.zeros((EXT, NV, 128), F32)
        acc0[...] = zeros
        acc1[...] = zeros
        acc2[...] = zeros
        for row in range(RL):
            flat = level * RL + row
            e = a_ref[flat]
            if not first:
                e = e - ext[row]
            hi, lo = split(e)
            out = nn(jnp.concatenate([hi, lo], axis=0), w_ref[flat])
            out = out[:NV] + out[NV:]
            adj_ref[flat] = out[:, 128:]
            i0, i1, i2 = [s_ref[flat * K + k] for k in range(K)]
            acc0[i0] += out[:, :128]
            acc1[i1] += out[:, :128]
            acc2[i2] += out[:, 128:]
        total = jnp.where(low_half((EXT, NV, 128)), acc0[...] + acc2[...], acc1[...])
        total = total + other_half(total)
        out_ref[...] = pack(total[W:W + RL])
        outgoing(pack(total[:W]), pack(total[W + RL:]))


def rows_kernel(x_ref, out_ref):
    spread = jnp.where(low_half((B * NV, 128)), 0.0, spread_matrix().astype(F32)).astype(BF16)
    gather = jnp.where(
        lax.broadcasted_iota(jnp.int32, (RL, RL * NV), 1) // NV
        == lax.broadcasted_iota(jnp.int32, (RL, RL * NV), 0), 1.0, 0.0).astype(BF16)
    mask = own_lane(RL * NV)

    def body(level, carry):
        x = x_ref[pl.ds(level * RL, RL)].reshape(RL * NV, 128)
        parts = split(x)
        for chunk in range(B * NV // 128):
            total = None
            for part in parts:
                wide = nt(part, spread[chunk * 128:(chunk + 1) * 128])
                kept = jnp.where(mask, wide, 0.0).astype(BF16)
                value = nn(gather, kept)
                total = value if total is None else total + value
            out_ref[level, :, pl.ds(chunk * 128, 128)] = total
        return carry

    lax.fori_loop(0, LV, body, 0)


def vspec():
    return pl.BlockSpec(memory_space=VMEM)


def sspec():
    return pl.BlockSpec(memory_space=SMEM)


def hspec():
    return pl.BlockSpec(memory_space=pl.ANY)


STATE = (ROWS, NV, 128)
OWN = (RL // 2, NV, 128)
SIDE = (W // 2, NV, 128)


def prepare(index, rhs, lower, dinv):
    return pl.pallas_call(
        prep_kernel,
        out_shape=(VMEM((ROWS, 2 * B, 256), BF16), VMEM(STATE, F32), SMEM(index.shape, jnp.int32)),
        in_specs=[sspec(), vspec(), hspec(), hspec()],
        out_specs=(vspec(), vspec(), sspec()),
        scratch_shapes=[
            VMEM((LV, K, RL, B * B), F32),
            VMEM((LV, RL, B * B), F32),
            VMEM((K + 1, 8 * B * B // 128, 128), F32),
            VMEM((2, 2, B, 128), F32),
            pltpu.SemaphoreType.DMA((2, LV)),
        ],
        compiler_params=pltpu.CompilerParams(vmem_limit_bytes=24 * MIB),
        name="prepare",
    )(index, in_vmem(rhs), lower, dinv)


def adjoint_state(index, relayed):
    return pl.pallas_call(
        adjoint_kernel,
        out_shape=VMEM(STATE, F32),
        in_specs=[sspec(), vspec()],
        out_specs=vspec(),
        compiler_params=pltpu.CompilerParams(vmem_limit_bytes=16 * MIB),
        name="adjoint_state",
    )(index, in_vmem(relayed))


def run_step(step, index, blocks, source, adjoint, own, left, right, sol, adj):
    turn = step % LV != LV - 1
    cross = step % LV != 0
    has_in = own is not None
    kernel_args = [in_smem(index), in_vmem(blocks), in_vmem(source), in_vmem(adjoint)]
    specs = [sspec(), vspec(), vspec(), vspec()]
    if has_in:
        kernel_args += [in_vmem(own), in_vmem(left), in_vmem(right)]
        specs += [vspec()] * 3
    aliases = {}
    if sol is not None:
        aliases = {len(kernel_args): 0, len(kernel_args) + 1: 1}
        kernel_args += [in_vmem(sol), in_vmem(adj)]
        specs += [vspec()] * 2

    def body(*refs):
        refs = list(refs)
        head, refs = refs[:4], refs[4:]
        arrivals = [None] * 3
        if has_in:
            arrivals, refs = refs[:3], refs[3:]
        held = [None] * 2
        if sol is not None:
            held, refs = refs[:2], refs[2:]
        step_kernel(step, cross, turn, *head, *arrivals, *held, *refs)

    return pl.pallas_call(
        body,
        out_shape=(VMEM(STATE, F32), VMEM(STATE, F32), VMEM(OWN, F32), VMEM(SIDE, F32), VMEM(SIDE, F32)),
        in_specs=specs,
        out_specs=(vspec(),) * 5,
        scratch_shapes=[VMEM((EXT, NV, 128), F32)] * 4,
        input_output_aliases=aliases,
        compiler_params=pltpu.CompilerParams(vmem_limit_bytes=16 * MIB),
        name="step%d" % step,
    )(*kernel_args)


def to_rows(state):
    return pl.pallas_call(
        rows_kernel,
        out_shape=jax.ShapeDtypeStruct((LV, RL, B * NV), F32),
        in_specs=[vspec()],
        out_specs=vspec(),
        compiler_params=pltpu.CompilerParams(vmem_limit_bytes=16 * MIB),
        name="to_rows",
    )(in_vmem(state))


def per_device(rhs, adjoint_owned, owner_of, columns, lower, dinv):
    cells = lax.axis_size("cell")
    sections = lax.axis_size("lvl")
    cell = lax.axis_index("cell")
    section = lax.axis_index("lvl")
    span = RL * cells
    owned = adjoint_owned.reshape(1, cells, B * NV)
    relayed = lax.all_to_all(owned, "cell", split_axis=1, concat_axis=1, tiled=True).reshape(ROWS, B * NV // 128, 128)
    position = cell * RL + jnp.arange(RL, dtype=jnp.int32)
    offset = (columns - position[None, :, None] + span // 2) % span - span // 2
    ext_index = jnp.clip(offset + jnp.arange(RL, dtype=jnp.int32)[None, :, None] + W, 0, EXT - 1)
    owner_row = owner_of % span
    owner_local = owner_of // span % LV * RL + owner_row % RL
    take = owner_local // cells * cells + owner_row // RL
    index = jnp.concatenate([
        ext_index.reshape(-1), take.reshape(-1),
        jnp.stack([section, cell % 2]).astype(jnp.int32),
    ])
    blocks, source, index = prepare(index, rhs, jnp.transpose(lower, (0, 2, 1, 3)), dinv)
    adjoint = adjoint_state(in_smem(index), relayed)

    near = [(i, i ^ 1) for i in range(cells)]
    far = [(i, (i + 1 if i % 2 else i - 1) % cells) for i in range(cells)]

    def handoff(x, rnd, by):
        moves = [(rnd, rnd + 1), (sections - 1 - rnd, sections - 2 - rnd)]
        pairs = [(a * cells + i, b * cells + (i + by) % cells) for a, b in moves for i in range(cells)]
        return lax.ppermute(x, ("lvl", "cell"), pairs)

    own = left = right = sol = adj = None
    for step in range(sections * LV):
        sol, adj, own, left, right = run_step(step, index, blocks, source, adjoint, own, left, right, sol, adj)
        if step == sections * LV - 1:
            break
        if step % LV != LV - 1:
            far_in = lax.ppermute(right, "cell", far)
            near_in = lax.ppermute(left, "cell", near)
            left, right = near_in, far_in
        else:
            rnd = step // LV
            from_right = handoff(left, rnd, -1)
            from_left = handoff(right, rnd, 1)
            own = handoff(own, rnd, 0)
            left, right = from_left, from_right
    return to_rows(sol), to_rows(adj)


def solution(mesh):
    return jax.shard_map(
        per_device,
        mesh=mesh,
        in_specs=(
            P("lvl", "cell", None),
            P("lvl", "cell", None),
            P("lvl", "cell"),
            P("lvl", "cell", None),
            P("lvl", "cell", None, None),
            P("lvl", "cell", None),
        ),
        out_specs=(P("lvl", "cell", None), P("lvl", "cell", None)),
        check_vma=False,
    )
```

```python
from functools import partial

import jax
import jax.numpy as jnp
from jax import lax
from jax.experimental import pallas as pl
from jax.experimental.pallas import tpu as pltpu
from jax.sharding import PartitionSpec as P

B = 64
NV = 16
K = 3
W = 8
LV = 4
RL = 16
ROWS = LV * RL
EXT = RL + 2 * W
VMEM = pltpu.VMEM
SMEM = pltpu.SMEM
F32 = jnp.float32
BF16 = jnp.bfloat16
MIB = 1 << 20


def in_vmem(x):
    return pltpu.with_memory_space_constraint(x, VMEM)


def in_hbm(x):
    return pltpu.with_memory_space_constraint(x, pltpu.HBM)


def in_smem(x):
    return pltpu.with_memory_space_constraint(x, SMEM)


def split(x):
    hi = x.astype(BF16)
    lo = (x - hi.astype(F32)).astype(BF16)
    return hi, lo


def nn(a, b):
    return jnp.dot(a, b, preferred_element_type=F32)


def nt(a, b):
    return lax.dot_general(a, b, (((1,), (1,)), ((), ())), preferred_element_type=F32)


def low_half(shape):
    return lax.broadcasted_iota(jnp.int32, shape, len(shape) - 1) % 128 < B


def other_half(x):
    return pltpu.roll(x, B, axis=x.ndim - 1)


def spread_matrix():
    row = lax.broadcasted_iota(jnp.int32, (B * NV, 128), 0) // NV
    col = lax.broadcasted_iota(jnp.int32, (B * NV, 128), 1) % B
    return jnp.where(row == col, 1.0, 0.0).astype(BF16)


def own_lane(rows):
    lane = lax.broadcasted_iota(jnp.int32, (rows, 128), 1) % NV
    vec = lax.broadcasted_iota(jnp.int32, (rows, 128), 0) % NV
    return lane == vec


def state_of_rows(load, spread, wide_hi, wide_lo):
    mask = own_lane(NV)
    for row in range(RL):
        for chunk in range(B * NV // 128):
            value = jnp.broadcast_to(load(row, chunk), (NV, 128))
            hi, lo = split(jnp.where(mask, value, 0.0))
            place = (pl.ds(row * NV, NV), pl.ds(chunk * 128, 128))
            wide_hi[place] = hi
            wide_lo[place] = lo
    out = nn(wide_hi[...], spread) + nn(wide_lo[...], spread)
    return out.reshape(RL, NV, 128)


def storage_level(part):
    section = lax.axis_index("lvl")
    return jnp.where(section < LV // 2, part, LV - 1 - part)


def blocks_kernel(part, first, *refs):
    if first:
        lower_hbm, dinv_hbm, rhs_hbm, owned_hbm, columns_hbm, owner_hbm, *refs = refs
        w_ref, r_ref, sent_ref, s_ref, *refs = refs
        low, din, tiles, both, sems, wide_hi, wide_lo, rhs_ref, table, turn, table_sem, *refs = refs
        owned_ref, columns_ref, owner_ref = refs
    else:
        lower_hbm, dinv_hbm, rhs_hbm, relayed_ref, s_ref, *refs = refs
        w_ref, r_ref, a_ref, *refs = refs
        low, din, tiles, both, sems, wide_hi, wide_lo, rhs_ref = refs
    level = storage_level(part)
    arrivals = []
    if first:
        arrivals += [
            pltpu.make_async_copy(columns_hbm, columns_ref, sems.at[3]),
            pltpu.make_async_copy(owner_hbm, owner_ref, sems.at[4]),
            pltpu.make_async_copy(owned_hbm, owned_ref, sems.at[5]),
        ]
    rhs_copy = pltpu.make_async_copy(rhs_hbm.at[level], rhs_ref, sems.at[2])
    copies = (
        pltpu.make_async_copy(lower_hbm.at[level], low, sems.at[0]),
        pltpu.make_async_copy(dinv_hbm.at[level], din, sems.at[1]),
    )
    for copy in (*arrivals, rhs_copy, *copies):
        copy.start()
    if first:
        for copy in arrivals:
            copy.wait()
        cells = lax.axis_size("cell")
        span = RL * cells
        shape = columns_ref.shape
        local = lax.broadcasted_iota(jnp.int32, shape, 2)
        offset = columns_ref[...] - local - lax.axis_index("cell") * RL
        offset = jnp.where(offset > span // 2, offset - span, offset)
        offset = jnp.where(offset < -(span // 2), offset + span, offset)
        place = jnp.clip(offset + local + W, 0, EXT - 1)
        for k in range(K):
            table[pl.ds(k * LV, LV), pl.ds(0, RL)] = place[k]
        owner = owner_ref[...]
        owner_row = owner % span
        owner_local = owner // span % LV * RL + owner_row % RL
        table[pl.ds(K * LV, LV), pl.ds(0, RL)] = owner_local // cells * cells + owner_row // RL
        table_copy = pltpu.make_async_copy(table, s_ref, table_sem)
        table_copy.start()
        for group in range(ROWS // 8):
            base = group % 2 * 8
            for chunk in range(B * NV // 128):
                turn[group, pl.ds(chunk * 8, 8), :] = owned_ref[group // 2, base:base + 8, chunk * 128:(chunk + 1) * 128]
            for row in range(8):
                sent_ref[group * 8 + row] = turn[group, pl.ds(row, B * NV // 128, stride=8), :]

    spread = spread_matrix()
    rhs_copy.wait()
    rhs = rhs_ref[...]

    def load_rhs(row, chunk):
        return rhs[row:row + 1, chunk * 128:(chunk + 1) * 128]

    r_ref[...] = state_of_rows(load_rhs, spread, wide_hi, wide_lo)
    if not first:
        def load_adjoint(row, chunk):
            return relayed_ref[s_ref[K * LV + level, row], pl.ds(chunk, 1), :]

        a_ref[...] = state_of_rows(load_adjoint, spread, wide_hi, wide_lo)

    left = low_half((B // 2, 128))
    left_wide = low_half((B, 128))
    for copy in copies:
        copy.wait()
    for half in range(2):
        start = half * 8
        for k in range(K + 1):
            for chunk in range(B * B // 128):
                lanes = pl.ds(chunk * 128, 128)
                value = low[k, pl.ds(start, 8), lanes] if k < K else din[pl.ds(start, 8), lanes]
                tiles[half, k, pl.ds(chunk * 8, 8), :] = value

    def row_blocks(half, row, slot):
        piece = [tiles[half, k, pl.ds(row, B // 2, stride=8), :] for k in range(K + 1)]
        turned = [other_half(p) for p in piece]
        both[slot, 0, pl.ds(0, B // 2, stride=2), :] = jnp.where(left, piece[0], turned[1])
        both[slot, 0, pl.ds(1, B // 2, stride=2), :] = jnp.where(left, turned[0], piece[1])
        both[slot, 1, pl.ds(0, B // 2, stride=2), :] = jnp.where(left, piece[2], turned[3])
        both[slot, 1, pl.ds(1, B // 2, stride=2), :] = jnp.where(left, turned[2], piece[3])
        first_tile, second = both[slot, 0], both[slot, 1]
        diag = other_half(second)[:, :B]
        diag_hi, diag_lo = split(diag)
        right_hi, right_lo = split(jnp.concatenate([first_tile, second], axis=1))
        top = nn(jnp.concatenate([diag_hi, diag_lo], axis=0), right_hi)
        product = top[:B] + top[B:] + nn(diag_hi, right_lo)
        tail = jnp.where(left_wide, product[:, 128:], second)
        hi, lo = split(jnp.concatenate([product[:, :128], tail], axis=1))
        w_ref[half * 8 + row] = jnp.concatenate([hi, lo], axis=0)

    for half in range(2):
        for row in range(8):
            row_blocks(half, row, half * 8 + row)


def adjoint_kernel(s_ref, relayed_ref, a_ref, wide_hi, wide_lo):
    level = storage_level(0)

    def load(row, chunk):
        return relayed_ref[s_ref[K * LV + level, row], pl.ds(chunk, 1), :]

    a_ref[...] = state_of_rows(load, spread_matrix(), wide_hi, wide_lo)


def pack(x):
    half = x.shape[0] // 2
    return jnp.where(low_half((half, NV, 128)), x[:half], x[half:])


def unpack(x):
    turned = other_half(x)
    left = low_half(x.shape)
    return jnp.concatenate([jnp.where(left, x, turned), jnp.where(left, turned, x)], axis=0)


def step_kernel(step, cross, turn, s_ref, w_ref, r_ref, a_ref, own_ref, left_ref, right_ref,
                res_ref, out_ref, outl_ref, outr_ref, ext, acc0, acc1, acc2):
    section = lax.axis_index("lvl")
    even = lax.axis_index("cell") % 2 == 0
    half = low_half((NV, 128))

    def incoming(do):
        if own_ref is None:
            return
        if not cross:
            do(left_ref, right_ref)
        else:
            pl.when(even)(lambda: do(right_ref, left_ref))
            pl.when(jnp.logical_not(even))(lambda: do(left_ref, right_ref))

    def outgoing(to_left, to_right):
        if not turn:
            outl_ref[...] = to_left
            outr_ref[...] = to_right
        else:
            @pl.when(even)
            def _():
                outl_ref[...] = to_right
                outr_ref[...] = to_left

            @pl.when(jnp.logical_not(even))
            def _():
                outl_ref[...] = to_left
                outr_ref[...] = to_right

    rnd, t = divmod(step, LV)
    first = step == 0

    @pl.when(section == rnd)
    def _():
        if not first:
            ext[pl.ds(W, RL)] = unpack(own_ref[...])

            def fill(from_left, from_right):
                ext[pl.ds(0, W)] = unpack(from_left[...])
                ext[pl.ds(W + RL, W)] = unpack(from_right[...])

            incoming(fill)
        results = []
        for row in range(RL):
            source = r_ref[row]
            if first:
                lhs = jnp.concatenate([jnp.zeros_like(source), jnp.where(half, 0.0, -source)], axis=1)
            else:
                x0, x1, x2 = [ext[s_ref[k * LV + t, row]] for k in range(K)]
                lhs = jnp.concatenate([jnp.where(half, x0, x1), jnp.where(half, x2, -source)], axis=1)
            hi, lo = split(lhs)
            out = nt(jnp.concatenate([hi, lo], axis=0), w_ref[row])
            out = out[:NV] + out[NV:]
            out = -(out + other_half(out))
            res_ref[row] = out
            results.append(out)
        x = jnp.stack(results)
        out_ref[...] = pack(x)
        outgoing(pack(x[:W]), pack(x[W:]))

    @pl.when(section == LV - 1 - rnd)
    def _():
        level = LV - 1 - t
        if not first:
            ext[pl.ds(0, RL)] = unpack(own_ref[...])

            def add(from_left, from_right):
                ext[pl.ds(0, W)] += unpack(from_left[...])
                ext[pl.ds(W, W)] += unpack(from_right[...])

            incoming(add)
        zeros = jnp.zeros((EXT, NV, 128), F32)
        acc0[...] = zeros
        acc1[...] = zeros
        acc2[...] = zeros
        for row in range(RL):
            e = a_ref[row]
            if not first:
                e = e - ext[row]
            hi, lo = split(e)
            out = nn(jnp.concatenate([hi, lo], axis=0), w_ref[row])
            out = out[:NV] + out[NV:]
            res_ref[row] = out[:, 128:]
            i0, i1, i2 = [s_ref[k * LV + level, row] for k in range(K)]
            acc0[i0] += out[:, :128]
            acc1[i1] += out[:, :128]
            acc2[i2] += out[:, 128:]
        total = jnp.where(low_half((EXT, NV, 128)), acc0[...] + acc2[...], acc1[...])
        total = total + other_half(total)
        out_ref[...] = pack(total[W:W + RL])
        outgoing(pack(total[:W]), pack(total[W + RL:]))


def rows_kernel(step, x_ref, *refs):
    sol_ref, adj_ref = refs[-2:]
    section = lax.axis_index("lvl")
    rnd, t = divmod(step, LV)

    def write(out_ref, level):
        spread = jnp.where(low_half((B * NV, 128)), 0.0, spread_matrix().astype(F32)).astype(BF16)
        mask = own_lane(RL * NV)
        hi, lo = split(x_ref[...].reshape(RL * NV, 128))
        for chunk in range(B * NV // 128):
            part = spread[chunk * 128:(chunk + 1) * 128]
            wide = jnp.where(mask, nt(hi, part) + nt(lo, part), 0.0)
            out_ref[level, :, pl.ds(chunk * 128, 128)] = jnp.sum(wide.reshape(RL, NV, 128), axis=1)

    pl.when(section == rnd)(lambda: write(sol_ref, t))
    pl.when(section == LV - 1 - rnd)(lambda: write(adj_ref, LV - 1 - t))


def vspec():
    return pl.BlockSpec(memory_space=VMEM)


def sspec():
    return pl.BlockSpec(memory_space=SMEM)


def hspec():
    return pl.BlockSpec(memory_space=pl.ANY)


STATE = (RL, NV, 128)
OWN = (RL // 2, NV, 128)
SIDE = (W // 2, NV, 128)
TABLE = ((K + 1) * LV, 128)
BLOCKS = (RL, 2 * B, 256)
OUT = (LV, RL, B * NV)


def params(mib):
    return pltpu.CompilerParams(vmem_limit_bytes=mib * MIB)


def cost(us):
    return pl.CostEstimate(flops=int(us * 1e9), bytes_accessed=int(us * 3e6), transcendentals=0)


def prepare(part, lower, dinv, rhs, *more):
    first = part == 0
    wide = VMEM((RL * NV, B * NV), BF16)
    scratch = [
        VMEM((K, RL, B * B), F32),
        VMEM((RL, B * B), F32),
        VMEM((2, K + 1, 8 * B * B // 128, 128), F32),
        VMEM((RL, 2, B, 128), F32),
        pltpu.SemaphoreType.DMA((6,)),
        wide,
        wide,
        VMEM((RL, B * NV), F32),
    ]
    shapes = [VMEM(BLOCKS, BF16), VMEM(STATE, F32)]
    specs = [hspec(), hspec(), hspec()]
    if first:
        shapes += [VMEM((ROWS, B * NV // 128, 128), F32), SMEM(TABLE, jnp.int32)]
        specs += [hspec()] * 3
        scratch += [VMEM(TABLE, jnp.int32), VMEM((ROWS // 8, B * NV // 16, 128), F32), pltpu.SemaphoreType.DMA]
        scratch += [VMEM(x.shape, x.dtype) for x in more]
        more = [in_hbm(x) for x in more]
    else:
        shapes += [VMEM(STATE, F32)]
        specs += [vspec(), sspec()]
        more = [in_vmem(more[0]), in_smem(more[1])]

    def body(*refs):
        blocks_kernel(part, first, *refs)
        if first:
            pltpu.make_async_copy(refs[-6], refs[9], refs[-4]).wait()

    return pl.pallas_call(
        body,
        out_shape=shapes,
        in_specs=specs,
        out_specs=[sspec() if first and i == 3 else vspec() for i in range(len(shapes))],
        scratch_shapes=scratch,
        compiler_params=params(12),
        cost_estimate=cost(2.5),
        name="prepare%d" % part,
    )(in_hbm(lower), in_hbm(dinv), in_hbm(rhs), *more)


def adjoint_state(table, relayed):
    wide = VMEM((RL * NV, B * NV), BF16)
    return pl.pallas_call(
        adjoint_kernel,
        out_shape=VMEM(STATE, F32),
        in_specs=[sspec(), vspec()],
        out_specs=vspec(),
        scratch_shapes=[wide, wide],
        compiler_params=params(8),
        cost_estimate=cost(0.5),
        name="adjoint_state",
    )(in_smem(table), in_vmem(relayed))


def run_step(step, table, blocks, source, adjoint, own, left, right):
    turn = step % LV != LV - 1
    cross = step % LV != 0
    has_in = own is not None
    kernel_args = [in_smem(table), in_vmem(blocks), in_vmem(source), in_vmem(adjoint)]
    specs = [sspec(), vspec(), vspec(), vspec()]
    if has_in:
        kernel_args += [in_vmem(own), in_vmem(left), in_vmem(right)]
        specs += [vspec()] * 3

    def body(*refs):
        head, refs = refs[:4], refs[4:]
        arrivals = [None] * 3
        if has_in:
            arrivals, refs = refs[:3], refs[3:]
        step_kernel(step, cross, turn, *head, *arrivals, *refs)

    return pl.pallas_call(
        body,
        out_shape=(VMEM(STATE, F32), VMEM(OWN, F32), VMEM(SIDE, F32), VMEM(SIDE, F32)),
        in_specs=specs,
        out_specs=(vspec(),) * 4,
        scratch_shapes=[VMEM((EXT, NV, 128), F32)] * 4,
        compiler_params=params(8),
        cost_estimate=cost(0.6),
        name="step%d" % step,
    )(*kernel_args)


def to_rows(step, result, outs):
    outs = [] if outs is None else [in_vmem(x) for x in outs]
    return pl.pallas_call(
        partial(rows_kernel, step),
        out_shape=(VMEM(OUT, F32), VMEM(OUT, F32)),
        in_specs=[vspec()] * (1 + len(outs)),
        out_specs=(vspec(), vspec()),
        input_output_aliases={1: 0, 2: 1} if outs else {},
        compiler_params=params(8),
        cost_estimate=cost(1.0),
        name="rows%d" % step,
    )(in_vmem(result), *outs)


def after(values, done):
    return lax.optimization_barrier((values, done))[0]


def per_device(rhs, adjoint_owned, owner_of, columns, lower, dinv):
    cells = lax.axis_size("cell")
    sections = lax.axis_size("lvl")
    lower = jnp.transpose(lower, (0, 2, 1, 3))
    columns = jnp.transpose(columns, (2, 0, 1))
    blocks, source, adjoint = ([None] * LV for _ in range(3))
    blocks[0], source[0], sent, table = prepare(0, lower, dinv, rhs, adjoint_owned, columns, owner_of)
    relayed = lax.all_to_all(sent.reshape(1, cells, B * NV), "cell", split_axis=1, concat_axis=1, tiled=True)
    relayed = relayed.reshape(ROWS, B * NV // 128, 128)
    adjoint[0] = adjoint_state(table, relayed)

    near = [(i, i ^ 1) for i in range(cells)]
    far = [(i, (i + 1 if i % 2 else i - 1) % cells) for i in range(cells)]

    def handoff(x, rnd, by):
        moves = [(rnd, rnd + 1), (sections - 1 - rnd, sections - 2 - rnd)]
        pairs = [(a * cells + i, b * cells + (i + by) % cells) for a, b in moves for i in range(cells)]
        return lax.ppermute(x, ("lvl", "cell"), pairs)

    own = left = right = outs = None
    for step in range(sections * LV):
        rnd, t = divmod(step, LV)
        part = t if rnd < LV // 2 else LV - 1 - t
        result, own, left, right = run_step(step, table, blocks[part], source[part], adjoint[part], own, left, right)
        if step < LV - 1:
            later = after((lower, dinv, rhs, relayed), left)
            blocks[step + 1], source[step + 1], adjoint[step + 1] = prepare(step + 1, *later, table)
        outs = to_rows(step, result, outs)
        if step == sections * LV - 1:
            break
        if t != LV - 1:
            far_in = lax.ppermute(right, "cell", far)
            near_in = lax.ppermute(left, "cell", near)
            left, right = near_in, far_in
        else:
            from_right = handoff(left, rnd, -1)
            from_left = handoff(right, rnd, 1)
            own = handoff(own, rnd, 0)
            left, right = from_left, from_right
    return outs


def solution(mesh):
    return jax.shard_map(
        per_device,
        mesh=mesh,
        in_specs=(
            P("lvl", "cell", None),
            P("lvl", "cell", None),
            P("lvl", "cell"),
            P("lvl", "cell", None),
            P("lvl", "cell", None, None),
            P("lvl", "cell", None),
        ),
        out_specs=(P("lvl", "cell", None), P("lvl", "cell", None)),
        check_vma=False,
    )
```

```python
from functools import partial

import jax
import jax.numpy as jnp
from jax import lax
from jax.experimental import pallas as pl
from jax.experimental.pallas import tpu as pltpu
from jax.sharding import PartitionSpec as P

B = 64
NV = 16
K = 3
W = 8
LV = 4
RL = 16
ROWS = LV * RL
EXT = RL + 2 * W
VMEM = pltpu.VMEM
SMEM = pltpu.SMEM
F32 = jnp.float32
BF16 = jnp.bfloat16
MIB = 1 << 20


def in_vmem(x):
    return pltpu.with_memory_space_constraint(x, VMEM)


def in_hbm(x):
    return pltpu.with_memory_space_constraint(x, pltpu.HBM)


def in_smem(x):
    return pltpu.with_memory_space_constraint(x, SMEM)


def split(x):
    hi = x.astype(BF16)
    lo = (x - hi.astype(F32)).astype(BF16)
    return hi, lo


def nn(a, b):
    return jnp.dot(a, b, preferred_element_type=F32)


def nt(a, b):
    return lax.dot_general(a, b, (((1,), (1,)), ((), ())), preferred_element_type=F32)


def low_half(shape):
    return lax.broadcasted_iota(jnp.int32, shape, len(shape) - 1) % 128 < B


def other_half(x):
    return pltpu.roll(x, B, axis=x.ndim - 1)


def spread_matrix():
    row = lax.broadcasted_iota(jnp.int32, (B * NV, 128), 0) // NV
    col = lax.broadcasted_iota(jnp.int32, (B * NV, 128), 1) % B
    return jnp.where(row == col, 1.0, 0.0).astype(BF16)


def own_lane(rows):
    lane = lax.broadcasted_iota(jnp.int32, (rows, 128), 1) % NV
    vec = lax.broadcasted_iota(jnp.int32, (rows, 128), 0) % NV
    return lane == vec


def state_of_rows(load, spread, wide_hi, wide_lo):
    mask = own_lane(NV)
    for row in range(RL):
        for chunk in range(B * NV // 128):
            value = jnp.broadcast_to(load(row, chunk), (NV, 128))
            hi, lo = split(jnp.where(mask, value, 0.0))
            place = (pl.ds(row * NV, NV), pl.ds(chunk * 128, 128))
            wide_hi[place] = hi
            wide_lo[place] = lo
    out = nn(wide_hi[...], spread) + nn(wide_lo[...], spread)
    return out.reshape(RL, NV, 128)


def storage_level(part):
    section = lax.axis_index("lvl")
    return jnp.where(section < LV // 2, part, LV - 1 - part)


def relay_kernel(owned_hbm, columns_hbm, owner_hbm, sent_hbm, s_ref,
                 table, turn, owned_ref, columns_ref, owner_ref, sent_rows, sems):
    arrivals = [
        pltpu.make_async_copy(owned_hbm, owned_ref, sems.at[0]),
        pltpu.make_async_copy(columns_hbm, columns_ref, sems.at[1]),
        pltpu.make_async_copy(owner_hbm, owner_ref, sems.at[2]),
    ]
    for copy in arrivals:
        copy.start()
    for copy in arrivals:
        copy.wait()
    for group in range(ROWS // 8):
        base = group % 2 * 8
        for chunk in range(B * NV // 128):
            turn[group, pl.ds(chunk * 8, 8), :] = owned_ref[group // 2, base:base + 8, chunk * 128:(chunk + 1) * 128]
        for row in range(8):
            sent_rows[group * 8 + row] = turn[group, pl.ds(row, B * NV // 128, stride=8), :]
    sent_copy = pltpu.make_async_copy(sent_rows, sent_hbm, sems.at[3])
    sent_copy.start()
    cells = lax.axis_size("cell")
    span = RL * cells
    local = lax.broadcasted_iota(jnp.int32, columns_ref.shape, 2)
    offset = columns_ref[...] - local - lax.axis_index("cell") * RL
    offset = jnp.where(offset > span // 2, offset - span, offset)
    offset = jnp.where(offset < -(span // 2), offset + span, offset)
    place = jnp.clip(offset + local + W, 0, EXT - 1)
    for k in range(K):
        table[pl.ds(k * LV, LV), pl.ds(0, RL)] = place[k]
    owner = owner_ref[...]
    owner_row = owner % span
    owner_local = owner // span % LV * RL + owner_row % RL
    table[pl.ds(K * LV, LV), pl.ds(0, RL)] = owner_local // cells * cells + owner_row // RL
    table_copy = pltpu.make_async_copy(table, s_ref, sems.at[4])
    table_copy.start()
    table_copy.wait()
    sent_copy.wait()


def blocks_kernel(part, lower_hbm, dinv_hbm, rhs_hbm, *refs):
    first = part == 0
    if first:
        w_ref, r_ref, low, din, tiles, both, sems, wide_hi, wide_lo, rhs_ref = refs
    else:
        relayed_ref, s_ref, w_ref, r_ref, a_ref, low, din, tiles, both, sems, wide_hi, wide_lo, rhs_ref = refs
    level = storage_level(part)
    rhs_copy = pltpu.make_async_copy(rhs_hbm.at[level], rhs_ref, sems.at[2])
    copies = (
        pltpu.make_async_copy(lower_hbm.at[level], low, sems.at[0]),
        pltpu.make_async_copy(dinv_hbm.at[level], din, sems.at[1]),
    )
    for copy in (rhs_copy, *copies):
        copy.start()
    spread = spread_matrix()
    if not first:
        def load_adjoint(row, chunk):
            return relayed_ref[s_ref[K * LV + level, row], pl.ds(chunk, 1), :]

        a_ref[...] = state_of_rows(load_adjoint, spread, wide_hi, wide_lo)

    rhs_copy.wait()
    rhs = rhs_ref[...]

    def load_rhs(row, chunk):
        return rhs[row:row + 1, chunk * 128:(chunk + 1) * 128]

    r_ref[...] = state_of_rows(load_rhs, spread, wide_hi, wide_lo)
    left = low_half((B // 2, 128))
    left_wide = low_half((B, 128))
    for copy in copies:
        copy.wait()
    for half in range(2):
        start = half * 8
        for k in range(K + 1):
            for chunk in range(B * B // 128):
                lanes = pl.ds(chunk * 128, 128)
                value = low[k, pl.ds(start, 8), lanes] if k < K else din[pl.ds(start, 8), lanes]
                tiles[half, k, pl.ds(chunk * 8, 8), :] = value

    def row_blocks(half, row, slot):
        piece = [tiles[half, k, pl.ds(row, B // 2, stride=8), :] for k in range(K + 1)]
        turned = [other_half(p) for p in piece]
        both[slot, 0, pl.ds(0, B // 2, stride=2), :] = jnp.where(left, piece[0], turned[1])
        both[slot, 0, pl.ds(1, B // 2, stride=2), :] = jnp.where(left, turned[0], piece[1])
        both[slot, 1, pl.ds(0, B // 2, stride=2), :] = jnp.where(left, piece[2], turned[3])
        both[slot, 1, pl.ds(1, B // 2, stride=2), :] = jnp.where(left, turned[2], piece[3])
        first_tile, second = both[slot, 0], both[slot, 1]
        diag = other_half(second)[:, :B]
        diag_hi, diag_lo = split(diag)
        right_hi, right_lo = split(jnp.concatenate([first_tile, second], axis=1))
        top = nn(jnp.concatenate([diag_hi, diag_lo], axis=0), right_hi)
        product = top[:B] + top[B:] + nn(diag_hi, right_lo)
        tail = jnp.where(left_wide, product[:, 128:], second)
        hi, lo = split(jnp.concatenate([product[:, :128], tail], axis=1))
        w_ref[half * 8 + row] = jnp.concatenate([hi, lo], axis=0)

    for half in range(2):
        for row in range(8):
            row_blocks(half, row, half * 8 + row)


def adjoint_kernel(s_ref, relayed_ref, a_ref, wide_hi, wide_lo):
    level = storage_level(0)

    def load(row, chunk):
        return relayed_ref[s_ref[K * LV + level, row], pl.ds(chunk, 1), :]

    a_ref[...] = state_of_rows(load, spread_matrix(), wide_hi, wide_lo)


def pack(x):
    half = x.shape[0] // 2
    return jnp.where(low_half((half, NV, 128)), x[:half], x[half:])


def unpack(x):
    turned = other_half(x)
    left = low_half(x.shape)
    return jnp.concatenate([jnp.where(left, x, turned), jnp.where(left, turned, x)], axis=0)


def is_even():
    return lax.axis_index("cell") % 2 == 0


def by_side(near, far, do):
    even = is_even()
    pl.when(even)(lambda: do(far, near))
    pl.when(jnp.logical_not(even))(lambda: do(near, far))


def forward_rows(pairs, lookup, ghosts=()):
    half = low_half((NV, 128))
    results = []
    for row, (block, source, places) in enumerate(pairs):
        last = jnp.zeros_like(source) if row in ghosts else -source
        if places is None:
            lhs = jnp.concatenate([jnp.zeros_like(source), jnp.where(half, 0.0, last)], axis=1)
        else:
            x0, x1, x2 = [lookup[i] for i in places]
            lhs = jnp.concatenate([jnp.where(half, x0, x1), jnp.where(half, x2, last)], axis=1)
        hi, lo = split(lhs)
        out = nt(jnp.concatenate([hi, lo], axis=0), block)
        out = out[:NV] + out[NV:]
        out = out + other_half(out)
        results.append(source - out if row in ghosts else -out)
    return results


def backward_rows(rows, window, accs):
    for acc in accs:
        acc[pl.ds(0, window)] = jnp.zeros((window, NV, 128), F32)
    results = []
    for block, value, (i0, i1, i2) in rows:
        hi, lo = split(value)
        out = nn(jnp.concatenate([hi, lo], axis=0), block)
        out = out[:NV] + out[NV:]
        results.append(out[:, 128:])
        accs[0][i0] += out[:, :128]
        accs[1][i1] += out[:, :128]
        accs[2][i2] += out[:, 128:]
    acc0, acc1, acc2 = [acc[pl.ds(0, window)] for acc in accs]
    total = jnp.where(low_half((window, NV, 128)), acc0 + acc2, acc1)
    return results, total + other_half(total)


def step_kernel(step, s_ref, w_ref, r_ref, a_ref, own_ref, near_ref, far_ref, res_ref, *refs):
    *outs, ext, acc0, acc1, acc2 = refs
    section = lax.axis_index("lvl")
    rnd, t = divmod(step, LV)
    first, handed = step == 0, t == 0

    def incoming(do):
        if handed:
            do(near_ref, far_ref)
        else:
            by_side(near_ref, far_ref, do)

    def outgoing(to_left, to_right, own):
        def put(near, far):
            if len(outs) == 1:
                outs[0][0] = near
                outs[0][1] = far
            else:
                outs[1][...] = near
                outs[2][...] = far

        if len(outs) == 3:
            outs[0][...] = own
        if len(outs) == 3 and t == LV - 1:
            put(to_left, to_right)
        else:
            even = is_even()
            pl.when(even)(lambda: put(to_right, to_left))
            pl.when(jnp.logical_not(even))(lambda: put(to_left, to_right))

    @pl.when(section == rnd)
    def _():
        if not first:
            ext[pl.ds(W, RL)] = unpack(own_ref[...])

            def fill(from_left, from_right):
                ext[pl.ds(0, W)] = unpack(from_left[...])
                ext[pl.ds(W + RL, W)] = unpack(from_right[...])

            incoming(fill)
        rows = [(w_ref[q], r_ref[q], None if first else [s_ref[k * LV + t, q] for k in range(K)])
                for q in range(RL)]
        x = jnp.stack(forward_rows(rows, ext))
        res_ref[...] = x
        if len(outs) == 1:
            outgoing(pack(x), pack(x), None)
        else:
            outgoing(pack(x[:W]), pack(x[W:]), pack(x))

    @pl.when(section == LV - 1 - rnd)
    def _():
        level = LV - 1 - t
        if not first:
            ext[pl.ds(0, RL)] = unpack(own_ref[...])

            def add(from_left, from_right):
                ext[pl.ds(0, W)] += unpack(from_left[...])
                ext[pl.ds(W, W)] += unpack(from_right[...])

            incoming(add)
        rows = [(w_ref[q], a_ref[q] if first else a_ref[q] - ext[q], [s_ref[k * LV + level, q] for k in range(K)])
                for q in range(RL)]
        results, total = backward_rows(rows, EXT, (acc0, acc1, acc2))
        res_ref[...] = jnp.stack(results)
        if len(outs) == 1:
            outgoing(pack(total[:RL]), pack(total[RL:]), None)
        else:
            outgoing(pack(total[:W]), pack(total[W + RL:]), pack(total[W:W + RL]))


def pair_kernel(rnd, t, s_ref, ghost_s, w0_ref, w1_ref, r0_ref, r1_ref, a0_ref, a1_ref, g_ref, gs_ref,
                own_near, own_far, near_ref, far_ref, res_ref, *refs):
    *outs, ext, ext2, acc0, acc1, acc2 = refs
    section = lax.axis_index("lvl")

    def outgoing(to_left, to_right):
        def put(near, far):
            if len(outs) == 1:
                outs[0][0] = near
                outs[0][1] = far
            else:
                outs[0][...] = near
                outs[1][...] = far

        even = is_even()
        pl.when(even)(lambda: put(to_right, to_left))
        pl.when(jnp.logical_not(even))(lambda: put(to_left, to_right))

    def window_rows(own_block, own_source, level):
        rows = []
        for q in range(EXT):
            if W <= q < W + RL:
                places = [s_ref[k * LV + level, q - W] + W for k in range(K)]
                rows.append((own_block[q - W], own_source[q - W], places))
            else:
                ghost = q if q < W else q - RL
                places = [ghost_s[t // 2 * 8 + k, ghost] for k in range(K)]
                rows.append((g_ref[ghost], gs_ref[ghost], places))
        return rows

    @pl.when(section == rnd)
    def _():
        ext[pl.ds(RL, RL)] = unpack(own_near[...])

        def fill(from_left, from_right):
            ext[pl.ds(0, RL)] = unpack(from_left[...])
            ext[pl.ds(2 * RL, RL)] = unpack(from_right[...])

        by_side(near_ref, far_ref, fill)
        ghost_rows = (*range(W), *range(W + RL, EXT))
        mid = forward_rows(window_rows(w0_ref, r0_ref, t), ext, ghost_rows)
        for q in range(EXT):
            ext2[q] = mid[q]
        res_ref[0] = jnp.stack(mid[W:W + RL])
        rows = [(w1_ref[q], r1_ref[q], [s_ref[k * LV + t + 1, q] for k in range(K)]) for q in range(RL)]
        x = jnp.stack(forward_rows(rows, ext2))
        res_ref[1] = x
        outgoing(pack(x), pack(x))

    @pl.when(section == LV - 1 - rnd)
    def _():
        level = LV - 1 - t

        def gather(own_left, own_right):
            ext[pl.ds(0, RL)] = unpack(own_left[...])
            ext[pl.ds(RL, RL)] = unpack(own_right[...])

        def add(from_left, from_right):
            ext[pl.ds(0, RL)] += unpack(from_left[...])
            ext[pl.ds(RL, RL)] += unpack(from_right[...])

        by_side(own_near, own_far, gather)
        by_side(near_ref, far_ref, add)
        rows = [(block, source - ext[q], places)
                for q, (block, source, places) in enumerate(window_rows(w0_ref, a0_ref, level))]
        results, total = backward_rows(rows, EXT + RL, (acc0, acc1, acc2))
        res_ref[0] = jnp.stack(results[W:W + RL])
        rows = [(w1_ref[q], a1_ref[q] - total[RL + q], [s_ref[k * LV + level - 1, q] for k in range(K)])
                for q in range(RL)]
        results, total = backward_rows(rows, EXT, (acc0, acc1, acc2))
        res_ref[1] = jnp.stack(results)
        outgoing(pack(total[:RL]), pack(total[RL:]))


def ghost_send_kernel(parts, s_ref, w0_ref, w1_ref, r0_ref, r1_ref, a0_ref, a1_ref, near_ref, far_ref):
    forward = lax.axis_index("lvl") >= LV // 2
    shift = jnp.where(is_even(), W, 0)
    sub = lax.broadcasted_iota(jnp.int32, (8, 128), 0)
    left = low_half((B // 2, 128))
    left8 = low_half((8, 128))
    for p, (w_ref, r_ref, a_ref) in enumerate(((w0_ref, r0_ref, a0_ref), (w1_ref, r1_ref, a1_ref))):
        level = storage_level(parts[p])
        for out_ref, base in ((near_ref, shift), (far_ref, W - shift)):
            for i in range(W):
                block = w_ref[base + i]
                block = block[:B].astype(F32) + block[B:].astype(F32)
                out_ref[p, i, pl.ds(0, B), :] = block[:, :128]
                third = block[:, 128:]
                out_ref[p, i, pl.ds(B, B // 2), :] = jnp.where(left, third[:B // 2], other_half(third[B // 2:]))
                direct, = forward_rows([(w_ref[base + i], r_ref[base + i], None)], None)
                value = jnp.where(forward, direct, a_ref[base + i])
                out_ref[p, i, pl.ds(96, 8), :] = jnp.where(left8, value[:8], value[8:])
                places = jnp.zeros((8, 128), F32)
                for k in range(K):
                    place = s_ref[k * LV + level, base + i].astype(F32)
                    places = jnp.where(sub == k, place, places)
                out_ref[p, i, pl.ds(104, 8), :] = places


def ghost_receive_kernel(near_ref, far_ref, g0_ref, g1_ref, gs0_ref, gs1_ref, t_ref, table, sem):
    shift = jnp.where(is_even(), W, 0)
    lane = lax.broadcasted_iota(jnp.int32, (8, 128), 1)
    left = low_half((B // 2, 128))
    for p, (g_ref, gs_ref) in enumerate(((g0_ref, gs0_ref), (g1_ref, gs1_ref))):
        places = jnp.zeros((8, 128), F32)
        for in_ref, base in ((near_ref, shift), (far_ref, W - shift)):
            for i in range(W):
                first = in_ref[p, i, pl.ds(0, B), :]
                packed = in_ref[p, i, pl.ds(B, B // 2), :]
                third = jnp.concatenate(
                    [jnp.where(left, packed, 0.0), jnp.where(left, other_half(packed), 0.0)], axis=0)
                hi, lo = split(jnp.concatenate([first, third], axis=1))
                g_ref[base + i] = jnp.concatenate([hi, lo], axis=0)
                gs_ref[base + i] = unpack(in_ref[p, i, pl.ds(96, 8), :].reshape(1, 8, 128)).reshape(NV, 128)
                places = jnp.where(lane == base + i, in_ref[p, i, pl.ds(104, 8), :], places)
        places = places.astype(jnp.int32) + jnp.where(lane < W, -W, RL + W)
        table[pl.ds(p * 8, 8), :] = jnp.clip(places, 0, EXT + RL - 1)
    copy = pltpu.make_async_copy(table, t_ref, sem)
    copy.start()
    copy.wait()


def rows_kernel(rnd, levels, x_ref, *refs):
    sol_ref, adj_ref = refs[-2:]
    section = lax.axis_index("lvl")

    def write(out_ref, place):
        spread = jnp.where(low_half((B * NV, 128)), 0.0, spread_matrix().astype(F32)).astype(BF16)
        mask = own_lane(RL * NV)
        for i, t in enumerate(levels):
            hi, lo = split(x_ref[pl.ds(i * RL, RL)].reshape(RL * NV, 128))
            for chunk in range(B * NV // 128):
                part = spread[chunk * 128:(chunk + 1) * 128]
                wide = jnp.where(mask, nt(hi, part) + nt(lo, part), 0.0)
                out_ref[place(t), :, pl.ds(chunk * 128, 128)] = jnp.sum(wide.reshape(RL, NV, 128), axis=1)

    pl.when(section == rnd)(lambda: write(sol_ref, lambda t: t))
    pl.when(section == LV - 1 - rnd)(lambda: write(adj_ref, lambda t: LV - 1 - t))


def vspec():
    return pl.BlockSpec(memory_space=VMEM)


def sspec():
    return pl.BlockSpec(memory_space=SMEM)


def hspec():
    return pl.BlockSpec(memory_space=pl.ANY)


STATE = (RL, NV, 128)
OWN = (RL // 2, NV, 128)
SIDE = (W // 2, NV, 128)
MSGS = (2, RL // 2, NV, 128)
GHOST = (2, W, 112, 128)
TABLE = ((K + 1) * LV, 128)
BLOCKS = (RL, 2 * B, 256)
SMEM_TABLE = SMEM(TABLE, jnp.int32)
OUT = (LV, RL, B * NV)


def params(mib):
    return pltpu.CompilerParams(vmem_limit_bytes=mib * MIB)


def cost(us):
    return pl.CostEstimate(flops=int(us * 1e9), bytes_accessed=int(us * 3e6), transcendentals=0)


def relay(owned, columns, owner):
    sent = (ROWS, B * NV // 128, 128)
    return pl.pallas_call(
        relay_kernel,
        out_shape=(pltpu.HBM(sent, F32), SMEM_TABLE),
        in_specs=[hspec()] * 3,
        out_specs=(hspec(), sspec()),
        scratch_shapes=[
            VMEM(TABLE, jnp.int32),
            VMEM((ROWS // 8, B * NV // 16, 128), F32),
            VMEM(owned.shape, F32),
            VMEM(columns.shape, jnp.int32),
            VMEM(owner.shape, jnp.int32),
            VMEM(sent, F32),
            pltpu.SemaphoreType.DMA((5,)),
        ],
        compiler_params=params(8),
        cost_estimate=cost(2.0),
        name="relay",
    )(in_hbm(owned), in_hbm(columns), in_hbm(owner))


def prepare(part, lower, dinv, rhs, *more):
    first = part == 0
    wide = VMEM((RL * NV, B * NV), BF16)
    scratch = [
        VMEM((K, RL, B * B), F32),
        VMEM((RL, B * B), F32),
        VMEM((2, K + 1, 8 * B * B // 128, 128), F32),
        VMEM((RL, 2, B, 128), F32),
        pltpu.SemaphoreType.DMA((3,)),
        wide,
        wide,
        VMEM((RL, B * NV), F32),
    ]
    shapes = [VMEM(BLOCKS, BF16), VMEM(STATE, F32)]
    specs = [hspec(), hspec(), hspec()]
    if not first:
        shapes += [VMEM(STATE, F32)]
        specs += [vspec(), sspec()]
        more = [in_vmem(more[0]), in_smem(more[1])]
    return pl.pallas_call(
        partial(blocks_kernel, part),
        out_shape=shapes,
        in_specs=specs,
        out_specs=[vspec()] * len(shapes),
        scratch_shapes=scratch,
        compiler_params=params(12),
        cost_estimate=cost(2.5),
        name="prepare%d" % part,
    )(in_hbm(lower), in_hbm(dinv), in_hbm(rhs), *more)


def adjoint_state(table, relayed):
    wide = VMEM((RL * NV, B * NV), BF16)
    return pl.pallas_call(
        adjoint_kernel,
        out_shape=VMEM(STATE, F32),
        in_specs=[sspec(), vspec()],
        out_specs=vspec(),
        scratch_shapes=[wide, wide],
        compiler_params=params(8),
        cost_estimate=cost(0.5),
        name="adjoint_state",
    )(in_smem(table), in_vmem(relayed))


def call(body, name, us, kernel_args, shapes, scratch=(), mib=8, **more):
    def place(x):
        return in_smem(x) if x.dtype == jnp.int32 and x.shape == TABLE else in_vmem(x)

    def spec(x):
        return sspec() if x.dtype == jnp.int32 and x.shape == TABLE else vspec()

    return pl.pallas_call(
        body,
        out_shape=tuple(shapes),
        in_specs=[spec(x) for x in kernel_args],
        out_specs=tuple(sspec() if isinstance(x, type(SMEM_TABLE)) and x.memory_space == SMEM else vspec() for x in shapes),
        scratch_shapes=list(scratch),
        compiler_params=params(mib),
        cost_estimate=cost(us),
        name=name,
        **more,
    )(*[place(x) for x in kernel_args])


def run_step(step, table, blocks, source, adjoint, own, near, far):
    kernel_args = [table, blocks, source, adjoint]
    if own is not None:
        kernel_args += [own, near, far]

    def body(*refs):
        head, refs = refs[:4], refs[4:]
        arrivals = [None] * 3
        if own is not None:
            arrivals, refs = refs[:3], refs[3:]
        step_kernel(step, *head, *arrivals, *refs)

    shapes = [VMEM(STATE, F32)]
    shapes += [VMEM(MSGS, F32)] if step == 2 * LV - 1 else [VMEM(OWN, F32), VMEM(SIDE, F32), VMEM(SIDE, F32)]
    return call(body, "step%d" % step, 0.6, kernel_args, shapes, [VMEM((EXT, NV, 128), F32)] * 4)


def run_pair(rnd, t, table, blocks, source, adjoint, ghost, arrivals):
    kernel_args = [table, ghost[-1], *blocks, *source, *adjoint, *ghost[:-1], *arrivals]
    shapes = [VMEM((2 * RL, NV, 128), F32)]
    shapes += [VMEM(OWN, F32)] * 2 if t == 0 else [VMEM(MSGS, F32)]

    def body(*refs):
        refs = list(refs)
        place = len(kernel_args)
        refs[place] = refs[place].reshape(2, RL, NV, 128)
        pair_kernel(rnd, t, *refs)

    scratch = [VMEM((EXT + RL, NV, 128), F32), VMEM((EXT, NV, 128), F32)] + [VMEM((EXT + RL, NV, 128), F32)] * 3
    return call(body, "pair%d_%d" % (rnd, t), 1.8, kernel_args, shapes, scratch)


def ghost_send(parts, table, blocks, source, adjoint):
    return call(partial(ghost_send_kernel, parts), "ghost_send", 0.5,
                [table, *blocks, *source, *adjoint], [VMEM(GHOST, F32)] * 2)


def ghost_receive(near, far):
    return call(ghost_receive_kernel, "ghost_receive", 0.5, [near, far],
                [VMEM(BLOCKS, BF16)] * 2 + [VMEM(STATE, F32)] * 2 + [SMEM_TABLE],
                [VMEM(TABLE, jnp.int32), pltpu.SemaphoreType.DMA])


def to_rows(rnd, levels, result, outs):
    outs = [] if outs is None else list(outs)
    return call(partial(rows_kernel, rnd, levels), "rows%d_%d" % (rnd, levels[0]), 0.5 * len(levels),
                [result, *outs], [VMEM(OUT, F32)] * 2, input_output_aliases={1: 0, 2: 1} if outs else {})


def after(values, done):
    return lax.optimization_barrier((values, done))[0]


def per_device(rhs, adjoint_owned, owner_of, columns, lower, dinv):
    cells = lax.axis_size("cell")
    sections = lax.axis_size("lvl")
    lower = jnp.transpose(lower, (0, 2, 1, 3))
    columns = jnp.transpose(columns, (2, 0, 1))
    blocks, source, adjoint = ([None] * LV for _ in range(3))
    sent, table = relay(adjoint_owned, columns, owner_of)
    relayed = lax.all_to_all(sent.reshape(1, cells, B * NV), "cell", split_axis=1, concat_axis=1, tiled=True)
    relayed = relayed.reshape(ROWS, B * NV // 128, 128)
    blocks[0], source[0] = prepare(0, lower, dinv, rhs)
    adjoint[0] = adjoint_state(table, relayed)

    near_of = [i ^ 1 for i in range(cells)]
    far_of = [(i + 1 if i % 2 else i - 1) % cells for i in range(cells)]

    def exchange(near, far):
        far_in = lax.ppermute(far, "cell", list(enumerate(far_of)))
        near_in = lax.ppermute(near, "cell", list(enumerate(near_of)))
        return near_in, far_in

    def shift_handoff(x, by):
        moves = [(0, 1), (sections - 1, sections - 2)]
        pairs = [(a * cells + i, b * cells + (i + by) % cells) for a, b in moves for i in range(cells)]
        return lax.ppermute(x, ("lvl", "cell"), pairs)

    def handoff(msgs, rnd):
        partner = [1, 0, 3, 2] if rnd % 2 == 0 else [3, 2, 1, 0]
        pairs = [(s * cells + i, partner[s] * cells + i) for s in range(sections) for i in range(cells)]
        return lax.ppermute(msgs, ("lvl", "cell"), pairs)

    own = near = far = outs = None
    for step in range(2 * LV):
        rnd, t = divmod(step, LV)
        result, *sent_out = run_step(step, table, blocks[t], source[t], adjoint[t], own, near, far)
        if step < LV - 1:
            later = after((lower, dinv, rhs, relayed), sent_out[-1])
            blocks[step + 1], source[step + 1], adjoint[step + 1] = prepare(step + 1, *later, table)
        if t < LV - 1:
            own = sent_out[0]
            near, far = exchange(*sent_out[1:])
            if step < LV - 1:
                near = after(near, blocks[step + 1])
        elif rnd == 0:
            own, to_left, to_right = sent_out
            own, near, far = shift_handoff(own, 0), shift_handoff(to_right, 1), shift_handoff(to_left, -1)
            parts = (LV - 1, 1)
            shared = after([[x[p] for p in parts] for x in (blocks, source, adjoint)], result)
            g0, g1, s0, s1, places = ghost_receive(*exchange(*ghost_send(parts, table, *shared)))
            ghosts = ((g0, s0, places), (g1, s1, places))
            near = after(near, ghosts)
        outs = to_rows(rnd, (t,), result, outs)
    msgs = sent_out[0]
    for rnd in range(LV // 2, sections):
        msgs = handoff(msgs, rnd - 1)
        own_near, own_far = msgs[0], msgs[1]
        for t in (0, 2):
            parts = (LV - 1 - t, LV - 2 - t)
            arrivals = (own_near, own_far, *exchange(own_near, own_far))
            picked = [[x[p] for p in parts] for x in (blocks, source, adjoint)]
            result, *sent_out = run_pair(rnd, t, table, *picked, ghosts[t // 2], arrivals)
            if t == 0:
                own_near, own_far = sent_out
            outs = to_rows(rnd, (t, t + 1), result, outs)
        msgs = sent_out[0]
    return outs


def solution(mesh):
    return jax.shard_map(
        per_device,
        mesh=mesh,
        in_specs=(
            P("lvl", "cell", None),
            P("lvl", "cell", None),
            P("lvl", "cell"),
            P("lvl", "cell", None),
            P("lvl", "cell", None, None),
            P("lvl", "cell", None),
        ),
        out_specs=(P("lvl", "cell", None), P("lvl", "cell", None)),
        check_vma=False,
    )
```

```python
from functools import partial

import jax
import jax.numpy as jnp
from jax import lax
from jax.experimental import pallas as pl
from jax.experimental.pallas import tpu as pltpu
from jax.sharding import PartitionSpec as P

B = 64
NV = 16
K = 3
W = 8
LV = 4
RL = 16
ROWS = LV * RL
EXT = RL + 2 * W
VMEM = pltpu.VMEM
SMEM = pltpu.SMEM
F32 = jnp.float32
BF16 = jnp.bfloat16
MIB = 1 << 20


def in_vmem(x):
    return pltpu.with_memory_space_constraint(x, VMEM)


def in_hbm(x):
    return pltpu.with_memory_space_constraint(x, pltpu.HBM)


def in_smem(x):
    return pltpu.with_memory_space_constraint(x, SMEM)


def split(x):
    hi = x.astype(BF16)
    lo = (x - hi.astype(F32)).astype(BF16)
    return hi, lo


def nn(a, b):
    return jnp.dot(a, b, preferred_element_type=F32)


def nt(a, b):
    return lax.dot_general(a, b, (((1,), (1,)), ((), ())), preferred_element_type=F32)


def low_half(shape):
    return lax.broadcasted_iota(jnp.int32, shape, len(shape) - 1) % 128 < B


def other_half(x):
    return pltpu.roll(x, B, axis=x.ndim - 1)


def spread_matrix():
    row = lax.broadcasted_iota(jnp.int32, (B * NV, 128), 0) // NV
    col = lax.broadcasted_iota(jnp.int32, (B * NV, 128), 1) % B
    return jnp.where(row == col, 1.0, 0.0).astype(BF16)


def own_lane(rows):
    lane = lax.broadcasted_iota(jnp.int32, (rows, 128), 1) % NV
    vec = lax.broadcasted_iota(jnp.int32, (rows, 128), 0) % NV
    return lane == vec


def state_of_rows(load, spread, wide_hi, wide_lo):
    mask = own_lane(NV)

    def group(start, carry):
        for row in range(8):
            for chunk in range(B * NV // 128):
                value = jnp.broadcast_to(load(start, row, chunk), (NV, 128))
                hi, lo = split(jnp.where(mask, value, 0.0))
                place = (pl.ds(pl.multiple_of((start * 8 + row) * NV, NV), NV), pl.ds(chunk * 128, 128))
                wide_hi[place] = hi
                wide_lo[place] = lo
        return carry

    lax.fori_loop(0, RL // 8, group, 0)
    out = nn(wide_hi[...], spread) + nn(wide_lo[...], spread)
    return out.reshape(RL, NV, 128)


def storage_level(part):
    section = lax.axis_index("lvl")
    return jnp.where(section < LV // 2, part, LV - 1 - part)


def relay_kernel(owned_hbm, columns_hbm, owner_hbm, sent_hbm, s_ref,
                 table, turn, owned_ref, columns_ref, owner_ref, sent_rows, sems):
    arrivals = [
        pltpu.make_async_copy(owned_hbm, owned_ref, sems.at[0]),
        pltpu.make_async_copy(columns_hbm, columns_ref, sems.at[1]),
        pltpu.make_async_copy(owner_hbm, owner_ref, sems.at[2]),
    ]
    for copy in arrivals:
        copy.start()
    for copy in arrivals:
        copy.wait()
    for group in range(ROWS // 8):
        base = group % 2 * 8
        for chunk in range(B * NV // 128):
            turn[group, pl.ds(chunk * 8, 8), :] = owned_ref[group // 2, base:base + 8, chunk * 128:(chunk + 1) * 128]
        for row in range(8):
            sent_rows[group * 8 + row] = turn[group, pl.ds(row, B * NV // 128, stride=8), :]
    sent_copy = pltpu.make_async_copy(sent_rows, sent_hbm, sems.at[3])
    sent_copy.start()
    cells = lax.axis_size("cell")
    span = RL * cells
    local = lax.broadcasted_iota(jnp.int32, columns_ref.shape, 2)
    offset = columns_ref[...] - local - lax.axis_index("cell") * RL
    offset = jnp.where(offset > span // 2, offset - span, offset)
    offset = jnp.where(offset < -(span // 2), offset + span, offset)
    place = jnp.clip(offset + local + W, 0, EXT - 1)
    for k in range(K):
        table[pl.ds(k * LV, LV), pl.ds(0, RL)] = place[k]
    owner = owner_ref[...]
    owner_row = owner % span
    owner_local = owner // span % LV * RL + owner_row % RL
    table[pl.ds(K * LV, LV), pl.ds(0, RL)] = owner_local // cells * cells + owner_row // RL
    table_copy = pltpu.make_async_copy(table, s_ref, sems.at[4])
    table_copy.start()
    table_copy.wait()
    sent_copy.wait()


def blocks_kernel(part, lower_hbm, dinv_hbm, rhs_hbm, w_ref, r_ref,
                  low, din, tiles, both, sems, wide_hi, wide_lo, rhs_ref):
    level = storage_level(part)
    rhs_copy = pltpu.make_async_copy(rhs_hbm.at[level], rhs_ref, sems.at[2])
    copies = (
        pltpu.make_async_copy(lower_hbm.at[level], low, sems.at[0]),
        pltpu.make_async_copy(dinv_hbm.at[level], din, sems.at[1]),
    )
    for copy in (rhs_copy, *copies):
        copy.start()
    spread = spread_matrix()
    rhs_copy.wait()

    def load_rhs(group, row, chunk):
        block = rhs_ref[pl.ds(pl.multiple_of(group * 8, 8), 8), pl.ds(chunk * 128, 128)]
        return block[row:row + 1]

    r_ref[...] = state_of_rows(load_rhs, spread, wide_hi, wide_lo)
    left = low_half((B // 2, 128))
    left_wide = low_half((B, 128))
    for copy in copies:
        copy.wait()
    def turn_half(half, carry):
        start = pl.multiple_of(half * 8, 8)
        for k in range(K + 1):
            for chunk in range(B * B // 128):
                lanes = pl.ds(chunk * 128, 128)
                value = low[k, pl.ds(start, 8), lanes] if k < K else din[pl.ds(start, 8), lanes]
                tiles[half, k, pl.ds(chunk * 8, 8), :] = value
        return carry

    lax.fori_loop(0, 2, turn_half, 0)

    def row_blocks(half, row, slot):
        piece = [tiles[half, k, pl.ds(row, B // 2, stride=8), :] for k in range(K + 1)]
        turned = [other_half(p) for p in piece]
        both[slot, 0, pl.ds(0, B // 2, stride=2), :] = jnp.where(left, piece[0], turned[1])
        both[slot, 0, pl.ds(1, B // 2, stride=2), :] = jnp.where(left, turned[0], piece[1])
        both[slot, 1, pl.ds(0, B // 2, stride=2), :] = jnp.where(left, piece[2], turned[3])
        both[slot, 1, pl.ds(1, B // 2, stride=2), :] = jnp.where(left, turned[2], piece[3])
        first_tile, second = both[slot, 0], both[slot, 1]
        diag = other_half(second)[:, :B]
        diag_hi, diag_lo = split(diag)
        right_hi, right_lo = split(jnp.concatenate([first_tile, second], axis=1))
        top = nn(jnp.concatenate([diag_hi, diag_lo], axis=0), right_hi)
        product = top[:B] + top[B:] + nn(diag_hi, right_lo)
        tail = jnp.where(left_wide, product[:, 128:], second)
        hi, lo = split(jnp.concatenate([product[:, :128], tail], axis=1))
        w_ref[half * 8 + row] = jnp.concatenate([hi, lo], axis=0)

    def four_rows(quarter, carry):
        for row in range(4):
            row_blocks(quarter // 2, quarter % 2 * 4 + row, row)
        return carry

    lax.fori_loop(0, 4, four_rows, 0)


def adjoint_kernel(parts, s_ref, relayed_ref, *refs):
    *outs, wide_hi, wide_lo = refs
    spread = spread_matrix()
    for part, a_ref in zip(parts, outs):
        level = storage_level(part)

        def load(group, row, chunk):
            return relayed_ref[s_ref[K * LV + level, group * 8 + row], pl.ds(chunk, 1), :]

        a_ref[...] = state_of_rows(load, spread, wide_hi, wide_lo)


def pack(x):
    half = x.shape[0] // 2
    return jnp.where(low_half((half, NV, 128)), x[:half], x[half:])


def unpack(x):
    turned = other_half(x)
    left = low_half(x.shape)
    return jnp.concatenate([jnp.where(left, x, turned), jnp.where(left, turned, x)], axis=0)


def is_even():
    return lax.axis_index("cell") % 2 == 0


def by_side(near, far, do):
    even = is_even()
    pl.when(even)(lambda: do(far, near))
    pl.when(jnp.logical_not(even))(lambda: do(near, far))


def forward_rows(pairs, lookup, ghosts=()):
    half = low_half((NV, 128))
    results = []
    for row, (block, source, places) in enumerate(pairs):
        last = jnp.zeros_like(source) if row in ghosts else -source
        if places is None:
            lhs = jnp.concatenate([jnp.zeros_like(source), jnp.where(half, 0.0, last)], axis=1)
        else:
            x0, x1, x2 = [lookup[i] for i in places]
            lhs = jnp.concatenate([jnp.where(half, x0, x1), jnp.where(half, x2, last)], axis=1)
        hi, lo = split(lhs)
        out = nt(jnp.concatenate([hi, lo], axis=0), block)
        out = out[:NV] + out[NV:]
        out = out + other_half(out)
        results.append(source - out if row in ghosts else -out)
    return results


def backward_rows(rows, window, accs):
    for acc in accs:
        acc[pl.ds(0, window)] = jnp.zeros((window, NV, 128), F32)
    results = []
    for block, value, (i0, i1, i2) in rows:
        hi, lo = split(value)
        out = nn(jnp.concatenate([hi, lo], axis=0), block)
        out = out[:NV] + out[NV:]
        results.append(out[:, 128:])
        accs[0][i0] += out[:, :128]
        accs[1][i1] += out[:, :128]
        accs[2][i2] += out[:, 128:]
    acc0, acc1, acc2 = [acc[pl.ds(0, window)] for acc in accs]
    total = jnp.where(low_half((window, NV, 128)), acc0 + acc2, acc1)
    return results, total + other_half(total)


def step_kernel(step, s_ref, w_ref, r_ref, a_ref, own_ref, near_ref, far_ref, res_ref, *refs):
    *outs, ext, acc0, acc1, acc2 = refs
    section = lax.axis_index("lvl")
    rnd, t = divmod(step, LV)
    first, handed = step == 0, t == 0

    def incoming(do):
        if handed:
            do(near_ref, far_ref)
        else:
            by_side(near_ref, far_ref, do)

    def outgoing(to_left, to_right, own):
        def put(near, far):
            if len(outs) == 1:
                outs[0][0] = near
                outs[0][1] = far
            else:
                outs[1][...] = near
                outs[2][...] = far

        if len(outs) == 3:
            outs[0][...] = own
        if len(outs) == 3 and t == LV - 1:
            put(to_left, to_right)
        else:
            even = is_even()
            pl.when(even)(lambda: put(to_right, to_left))
            pl.when(jnp.logical_not(even))(lambda: put(to_left, to_right))

    @pl.when(section == rnd)
    def _():
        if not first:
            ext[pl.ds(W, RL)] = unpack(own_ref[...])

            def fill(from_left, from_right):
                ext[pl.ds(0, W)] = unpack(from_left[...])
                ext[pl.ds(W + RL, W)] = unpack(from_right[...])

            incoming(fill)
        rows = [(w_ref[q], r_ref[q], None if first else [s_ref[k * LV + t, q] for k in range(K)])
                for q in range(RL)]
        x = jnp.stack(forward_rows(rows, ext))
        res_ref[...] = x
        if len(outs) == 1:
            outgoing(pack(x), pack(x), None)
        else:
            outgoing(pack(x[:W]), pack(x[W:]), pack(x))

    @pl.when(section == LV - 1 - rnd)
    def _():
        level = LV - 1 - t
        if not first:
            ext[pl.ds(0, RL)] = unpack(own_ref[...])

            def add(from_left, from_right):
                ext[pl.ds(0, W)] += unpack(from_left[...])
                ext[pl.ds(W, W)] += unpack(from_right[...])

            incoming(add)
        rows = [(w_ref[q], a_ref[q] if first else a_ref[q] - ext[q], [s_ref[k * LV + level, q] for k in range(K)])
                for q in range(RL)]
        results, total = backward_rows(rows, EXT, (acc0, acc1, acc2))
        res_ref[...] = jnp.stack(results)
        if len(outs) == 1:
            outgoing(pack(total[:RL]), pack(total[RL:]), None)
        else:
            outgoing(pack(total[:W]), pack(total[W + RL:]), pack(total[W:W + RL]))


def pair_kernel(rnd, t, s_ref, ghost_s, w0_ref, w1_ref, r0_ref, r1_ref, a0_ref, a1_ref, g_ref, gs_ref,
                own_near, own_far, near_ref, far_ref, res0_ref, res1_ref, *refs):
    *outs, ext, ext2, acc0, acc1, acc2 = refs
    section = lax.axis_index("lvl")

    def outgoing(to_left, to_right):
        def put(near, far):
            if len(outs) == 1:
                outs[0][0] = near
                outs[0][1] = far
            else:
                outs[0][...] = near
                outs[1][...] = far

        even = is_even()
        pl.when(even)(lambda: put(to_right, to_left))
        pl.when(jnp.logical_not(even))(lambda: put(to_left, to_right))

    def window_rows(own_block, own_source, level):
        rows = []
        for q in range(EXT):
            if W <= q < W + RL:
                places = [s_ref[k * LV + level, q - W] + W for k in range(K)]
                rows.append((own_block[q - W], own_source[q - W], places))
            else:
                ghost = q if q < W else q - RL
                places = [ghost_s[k, ghost] for k in range(K)]
                rows.append((g_ref[ghost], gs_ref[ghost], places))
        return rows

    @pl.when(section == rnd)
    def _():
        ext[pl.ds(RL, RL)] = unpack(own_near[...])

        def fill(from_left, from_right):
            ext[pl.ds(0, RL)] = unpack(from_left[...])
            ext[pl.ds(2 * RL, RL)] = unpack(from_right[...])

        by_side(near_ref, far_ref, fill)
        ghost_rows = (*range(W), *range(W + RL, EXT))
        mid = forward_rows(window_rows(w0_ref, r0_ref, t), ext, ghost_rows)
        for q in range(EXT):
            ext2[q] = mid[q]
        res0_ref[...] = jnp.stack(mid[W:W + RL])
        rows = [(w1_ref[q], r1_ref[q], [s_ref[k * LV + t + 1, q] for k in range(K)]) for q in range(RL)]
        x = jnp.stack(forward_rows(rows, ext2))
        res1_ref[...] = x
        outgoing(pack(x), pack(x))

    @pl.when(section == LV - 1 - rnd)
    def _():
        level = LV - 1 - t

        def gather(own_left, own_right):
            ext[pl.ds(0, RL)] = unpack(own_left[...])
            ext[pl.ds(RL, RL)] = unpack(own_right[...])

        def add(from_left, from_right):
            ext[pl.ds(0, RL)] += unpack(from_left[...])
            ext[pl.ds(RL, RL)] += unpack(from_right[...])

        by_side(own_near, own_far, gather)
        by_side(near_ref, far_ref, add)
        rows = [(block, source - ext[q], places)
                for q, (block, source, places) in enumerate(window_rows(w0_ref, a0_ref, level))]
        results, total = backward_rows(rows, EXT + RL, (acc0, acc1, acc2))
        res0_ref[...] = jnp.stack(results[W:W + RL])
        rows = [(w1_ref[q], a1_ref[q] - total[RL + q], [s_ref[k * LV + level - 1, q] for k in range(K)])
                for q in range(RL)]
        results, total = backward_rows(rows, EXT, (acc0, acc1, acc2))
        res1_ref[...] = jnp.stack(results)
        outgoing(pack(total[:RL]), pack(total[RL:]))


def ghost_send_kernel(part, s_ref, w_ref, r_ref, a_ref, near_ref, far_ref):
    forward = lax.axis_index("lvl") >= LV // 2
    shift = jnp.where(is_even(), W, 0)
    sub = lax.broadcasted_iota(jnp.int32, (8, 128), 0)
    left = low_half((B // 2, 128))
    left8 = low_half((8, 128))
    level = storage_level(part)
    for out_ref, base in ((near_ref, shift), (far_ref, W - shift)):

        def one(i, carry):
            block = w_ref[base + i]
            block = block[:B].astype(F32) + block[B:].astype(F32)
            out_ref[i, pl.ds(0, B), :] = block[:, :128]
            third = block[:, 128:]
            out_ref[i, pl.ds(B, B // 2), :] = jnp.where(left, third[:B // 2], other_half(third[B // 2:]))
            direct, = forward_rows([(w_ref[base + i], r_ref[base + i], None)], None)
            value = jnp.where(forward, direct, a_ref[base + i])
            out_ref[i, pl.ds(96, 8), :] = jnp.where(left8, value[:8], value[8:])
            places = jnp.zeros((8, 128), F32)
            for k in range(K):
                place = s_ref[k * LV + level, base + i].astype(F32)
                places = jnp.where(sub == k, place, places)
            out_ref[i, pl.ds(104, 8), :] = places
            return carry

        lax.fori_loop(0, W, one, 0, unroll=2)


def ghost_receive_kernel(near_ref, far_ref, g_ref, gs_ref, t_ref, table, sem):
    shift = jnp.where(is_even(), W, 0)
    lane = lax.broadcasted_iota(jnp.int32, (8, 128), 1)
    left = low_half((B // 2, 128))
    places = jnp.zeros((8, 128), F32)
    for in_ref, base in ((near_ref, shift), (far_ref, W - shift)):

        def one(i, places):
            first = in_ref[i, pl.ds(0, B), :]
            packed = in_ref[i, pl.ds(B, B // 2), :]
            third = jnp.concatenate(
                [jnp.where(left, packed, 0.0), jnp.where(left, other_half(packed), 0.0)], axis=0)
            hi, lo = split(jnp.concatenate([first, third], axis=1))
            g_ref[base + i] = jnp.concatenate([hi, lo], axis=0)
            gs_ref[base + i] = unpack(in_ref[i, pl.ds(96, 8), :].reshape(1, 8, 128)).reshape(NV, 128)
            return jnp.where(lane == base + i, in_ref[i, pl.ds(104, 8), :], places)

        places = lax.fori_loop(0, W, one, places, unroll=2)
    places = places.astype(jnp.int32) + jnp.where(lane < W, -W, RL + W)
    table[pl.ds(0, 8), :] = jnp.clip(places, 0, EXT + RL - 1)
    table[pl.ds(8, 8), :] = jnp.zeros((8, 128), jnp.int32)
    copy = pltpu.make_async_copy(table, t_ref, sem)
    copy.start()
    copy.wait()


def rows_kernel(rnd, levels, *refs):
    *refs, sol_ref, adj_ref, spread_ref, lines = refs
    results = refs[:len(levels)]
    section = lax.axis_index("lvl")
    forward = section == rnd

    @pl.when(jnp.logical_or(forward, section == LV - 1 - rnd))
    def _():
        spread = jnp.where(low_half((B * NV, 128)), 0.0, spread_matrix().astype(F32)).astype(BF16)
        spread_ref[...] = spread.reshape(B * NV // 128, 128, 128)
        mask = own_lane(RL * NV)
        for t, x in zip(levels, results):
            hi, lo = split(x[...].reshape(RL * NV, 128))

            def one(chunk, carry):
                part = spread_ref[chunk]
                wide = jnp.where(mask, nt(hi, part) + nt(lo, part), 0.0)
                lines[chunk] = jnp.sum(wide.reshape(RL, NV, 128), axis=1)
                return carry

            lax.fori_loop(0, B * NV // 128, one, 0, unroll=8 if rnd == LV - 1 else 2)
            for chunk in range(B * NV // 128):
                lanes = pl.ds(chunk * 128, 128)

                @pl.when(forward)
                def _():
                    sol_ref[t, :, lanes] = lines[chunk]

                @pl.when(jnp.logical_not(forward))
                def _():
                    adj_ref[LV - 1 - t, :, lanes] = lines[chunk]


def vspec():
    return pl.BlockSpec(memory_space=VMEM)


def sspec():
    return pl.BlockSpec(memory_space=SMEM)


def hspec():
    return pl.BlockSpec(memory_space=pl.ANY)


STATE = (RL, NV, 128)
OWN = (RL // 2, NV, 128)
SIDE = (W // 2, NV, 128)
MSGS = (2, RL // 2, NV, 128)
GHOST = (W, 112, 128)
GHOST_STEPS = {1: 3, 2: 1}
TABLE = ((K + 1) * LV, 128)
BLOCKS = (RL, 2 * B, 256)
SMEM_TABLE = SMEM(TABLE, jnp.int32)
OUT = (LV, RL, B * NV)


def params(mib):
    return pltpu.CompilerParams(vmem_limit_bytes=mib * MIB)


def cost(us):
    return pl.CostEstimate(flops=int(us * 1e9), bytes_accessed=int(us * 3e6), transcendentals=0)


def relay(owned, columns, owner):
    sent = (ROWS, B * NV // 128, 128)
    return pl.pallas_call(
        relay_kernel,
        out_shape=(pltpu.HBM(sent, F32), SMEM_TABLE),
        in_specs=[hspec()] * 3,
        out_specs=(hspec(), sspec()),
        scratch_shapes=[
            VMEM(TABLE, jnp.int32),
            VMEM((ROWS // 8, B * NV // 16, 128), F32),
            VMEM(owned.shape, F32),
            VMEM(columns.shape, jnp.int32),
            VMEM(owner.shape, jnp.int32),
            VMEM(sent, F32),
            pltpu.SemaphoreType.DMA((5,)),
        ],
        compiler_params=params(8),
        cost_estimate=cost(2.0),
        name="relay",
    )(in_hbm(owned), in_hbm(columns), in_hbm(owner))


def prepare(part, lower, dinv, rhs):
    wide = VMEM((RL * NV, B * NV), BF16)
    scratch = [
        VMEM((K, RL, B * B), F32),
        VMEM((RL, B * B), F32),
        VMEM((2, K + 1, 8 * B * B // 128, 128), F32),
        VMEM((4, 2, B, 128), F32),
        pltpu.SemaphoreType.DMA((3,)),
        wide,
        wide,
        VMEM((RL, B * NV), F32),
    ]
    shapes = [VMEM(BLOCKS, BF16), VMEM(STATE, F32)]
    specs = [hspec(), hspec(), hspec()]
    return pl.pallas_call(
        partial(blocks_kernel, part),
        out_shape=shapes,
        in_specs=specs,
        out_specs=[vspec()] * len(shapes),
        scratch_shapes=scratch,
        compiler_params=params(12),
        cost_estimate=cost(2.5),
        name="prepare%d" % part,
    )(in_hbm(lower), in_hbm(dinv), in_hbm(rhs))


def adjoint_state(parts, table, relayed):
    wide = VMEM((RL * NV, B * NV), BF16)
    return call(partial(adjoint_kernel, parts), "adjoint_state", 0.6 * len(parts), [table, relayed],
                [VMEM(STATE, F32)] * len(parts), [wide, wide])


def call(body, name, us, kernel_args, shapes, scratch=(), mib=8, **more):
    def place(x):
        return in_smem(x) if x.dtype == jnp.int32 and x.shape == TABLE else in_vmem(x)

    def spec(x):
        return sspec() if x.dtype == jnp.int32 and x.shape == TABLE else vspec()

    return pl.pallas_call(
        body,
        out_shape=tuple(shapes),
        in_specs=[spec(x) for x in kernel_args],
        out_specs=tuple(sspec() if isinstance(x, type(SMEM_TABLE)) and x.memory_space == SMEM else vspec() for x in shapes),
        scratch_shapes=list(scratch),
        compiler_params=params(mib),
        cost_estimate=cost(us),
        name=name,
        **more,
    )(*[place(x) for x in kernel_args])


def run_step(step, table, blocks, source, adjoint, own, near, far):
    kernel_args = [table, blocks, source, adjoint]
    if own is not None:
        kernel_args += [own, near, far]

    def body(*refs):
        head, refs = refs[:4], refs[4:]
        arrivals = [None] * 3
        if own is not None:
            arrivals, refs = refs[:3], refs[3:]
        step_kernel(step, *head, *arrivals, *refs)

    shapes = [VMEM(STATE, F32)]
    shapes += [VMEM(MSGS, F32)] if step == 2 * LV - 1 else [VMEM(OWN, F32), VMEM(SIDE, F32), VMEM(SIDE, F32)]
    return call(body, "step%d" % step, 0.6, kernel_args, shapes, [VMEM((EXT, NV, 128), F32)] * 4)


def run_pair(rnd, t, table, blocks, source, adjoint, ghost, arrivals):
    kernel_args = [table, ghost[-1], *blocks, *source, *adjoint, *ghost[:-1], *arrivals]
    shapes = [VMEM(STATE, F32)] * 2
    shapes += [VMEM(OWN, F32)] * 2 if t == 0 else [VMEM(MSGS, F32)]

    scratch = [VMEM((EXT + RL, NV, 128), F32), VMEM((EXT, NV, 128), F32)] + [VMEM((EXT + RL, NV, 128), F32)] * 3
    return call(partial(pair_kernel, rnd, t), "pair%d_%d" % (rnd, t), 1.8, kernel_args, shapes, scratch)


def ghost_send(part, table, blocks, source, adjoint):
    return call(partial(ghost_send_kernel, part), "ghost_send", 0.5,
                [table, blocks, source, adjoint], [VMEM(GHOST, F32)] * 2)


def ghost_receive(near, far):
    return call(ghost_receive_kernel, "ghost_receive", 0.5, [near, far],
                [VMEM(BLOCKS, BF16), VMEM(STATE, F32), SMEM_TABLE],
                [VMEM(TABLE, jnp.int32), pltpu.SemaphoreType.DMA])


def to_rows(rnd, levels, results, outs):
    outs = [] if outs is None else list(outs)
    place = len(results)
    return call(partial(rows_kernel, rnd, levels), "rows%d_%d" % (rnd, levels[0]), 0.6 * len(levels),
                [*results, *outs], [VMEM(OUT, F32)] * 2,
                [VMEM((B * NV // 128, 128, 128), BF16), VMEM((B * NV // 128, RL, 128), F32)],
                input_output_aliases={place: 0, place + 1: 1} if outs else {})


def after(values, done):
    return lax.optimization_barrier((values, done))[0]


def per_device(rhs, adjoint_owned, owner_of, columns, lower, dinv):
    cells = lax.axis_size("cell")
    sections = lax.axis_size("lvl")
    lower = jnp.transpose(lower, (0, 2, 1, 3))
    columns = jnp.transpose(columns, (2, 0, 1))
    blocks, source, adjoint = ([None] * LV for _ in range(3))
    sent, table = relay(adjoint_owned, columns, owner_of)
    relayed = lax.all_to_all(sent.reshape(1, cells, B * NV), "cell", split_axis=1, concat_axis=1, tiled=True)
    relayed = relayed.reshape(ROWS, B * NV // 128, 128)
    for part in range(LV):
        blocks[part], source[part] = prepare(part, *after((lower, dinv, rhs), sent))
    adjoint[0], = adjoint_state((0,), table, relayed)

    near_of = [i ^ 1 for i in range(cells)]
    far_of = [(i + 1 if i % 2 else i - 1) % cells for i in range(cells)]

    def exchange(near, far):
        far_in = lax.ppermute(far, "cell", list(enumerate(far_of)))
        near_in = lax.ppermute(near, "cell", list(enumerate(near_of)))
        return near_in, far_in

    def shift_handoff(x, by):
        moves = [(0, 1), (sections - 1, sections - 2)]
        pairs = [(a * cells + i, b * cells + (i + by) % cells) for a, b in moves for i in range(cells)]
        return lax.ppermute(x, ("lvl", "cell"), pairs)

    def handoff(msgs, rnd):
        partner = [1, 0, 3, 2] if rnd % 2 == 0 else [3, 2, 1, 0]
        pairs = [(s * cells + i, partner[s] * cells + i) for s in range(sections) for i in range(cells)]
        return lax.ppermute(msgs, ("lvl", "cell"), pairs)

    ghosts = {}
    own = near = far = outs = None
    for step in range(2 * LV):
        rnd, t = divmod(step, LV)
        result, *sent_out = run_step(step, table, blocks[t], source[t], adjoint[t], own, near, far)
        if step == 0:
            adjoint[1:] = adjoint_state((1, 2, 3), table, after(relayed, sent_out[-1]))
        if step in GHOST_STEPS:
            part = GHOST_STEPS[step]
            shared = after((blocks[part], source[part], adjoint[part]), sent_out[-1])
            ghosts[part] = ghost_receive(*exchange(*ghost_send(part, table, *shared)))
        if t < LV - 1:
            own = sent_out[0]
            near, far = exchange(*sent_out[1:])
        elif rnd == 0:
            own, to_left, to_right = sent_out
            own, near, far = shift_handoff(own, 0), shift_handoff(to_right, 1), shift_handoff(to_left, -1)
        results = [result] if t == 0 else [*results, result]
        if t == LV - 1:
            outs = to_rows(rnd, tuple(range(LV)), results, outs)
    msgs = sent_out[0]
    for rnd in range(LV // 2, sections):
        msgs = handoff(msgs, rnd - 1)
        own_near, own_far = msgs[0], msgs[1]
        for t in (0, 2):
            parts = (LV - 1 - t, LV - 2 - t)
            arrivals = (own_near, own_far, *exchange(own_near, own_far))
            picked = [[x[p] for p in parts] for x in (blocks, source, adjoint)]
            first, second, *sent_out = run_pair(rnd, t, table, *picked, ghosts[parts[0]], arrivals)
            if t == 0:
                own_near, own_far = sent_out
            outs = to_rows(rnd, (t, t + 1), (first, second), outs)
        msgs = sent_out[0]
    return outs


def solution(mesh):
    return jax.shard_map(
        per_device,
        mesh=mesh,
        in_specs=(
            P("lvl", "cell", None),
            P("lvl", "cell", None),
            P("lvl", "cell"),
            P("lvl", "cell", None),
            P("lvl", "cell", None, None),
            P("lvl", "cell", None),
        ),
        out_specs=(P("lvl", "cell", None), P("lvl", "cell", None)),
        check_vma=False,
    )
```

```python
from functools import partial

import jax
import jax.numpy as jnp
from jax import lax
from jax.experimental import pallas as pl
from jax.experimental.pallas import tpu as pltpu
from jax.sharding import PartitionSpec as P

B = 64
NV = 16
K = 3
W = 8
LV = 4
RL = 16
ROWS = LV * RL
EXT = RL + 2 * W
VMEM = pltpu.VMEM
SMEM = pltpu.SMEM
F32 = jnp.float32
BF16 = jnp.bfloat16
MIB = 1 << 20


def in_vmem(x):
    return pltpu.with_memory_space_constraint(x, VMEM)


def in_hbm(x):
    return pltpu.with_memory_space_constraint(x, pltpu.HBM)


def in_smem(x):
    return pltpu.with_memory_space_constraint(x, SMEM)


def split(x):
    hi = x.astype(BF16)
    lo = (x - hi.astype(F32)).astype(BF16)
    return hi, lo


def nn(a, b):
    return jnp.dot(a, b, preferred_element_type=F32)


def nt(a, b):
    return lax.dot_general(a, b, (((1,), (1,)), ((), ())), preferred_element_type=F32)


def low_half(shape):
    return lax.broadcasted_iota(jnp.int32, shape, len(shape) - 1) % 128 < B


def other_half(x):
    return pltpu.roll(x, B, axis=x.ndim - 1)


def spread_matrix():
    row = lax.broadcasted_iota(jnp.int32, (B * NV, 128), 0) // NV
    col = lax.broadcasted_iota(jnp.int32, (B * NV, 128), 1) % B
    return jnp.where(row == col, 1.0, 0.0).astype(BF16)


def own_lane(rows):
    lane = lax.broadcasted_iota(jnp.int32, (rows, 128), 1) % NV
    vec = lax.broadcasted_iota(jnp.int32, (rows, 128), 0) % NV
    return lane == vec


def state_of_rows(load, wide_hi, wide_lo):
    mask = own_lane(NV)

    def one(row, carry):
        block = load(row)
        for chunk in range(B * NV // 128):
            value = jnp.broadcast_to(block[chunk:chunk + 1], (NV, 128))
            hi, lo = split(jnp.where(mask, value, 0.0))
            place = (pl.ds(pl.multiple_of(row * NV, NV), NV), pl.ds(chunk * 128, 128))
            wide_hi[place] = hi
            wide_lo[place] = lo
        return carry

    lax.fori_loop(0, RL, one, 0, unroll=2)
    row = lax.broadcasted_iota(jnp.int32, (256, 128), 0) // NV
    col = lax.broadcasted_iota(jnp.int32, (256, 128), 1) % B

    def add(part, total):
        spread = jnp.where(row + part * (256 // NV) == col, 1.0, 0.0).astype(BF16)
        lanes = pl.ds(pl.multiple_of(part * 256, 256), 256)
        return total + nn(wide_hi[:, lanes], spread) + nn(wide_lo[:, lanes], spread)

    out = lax.fori_loop(0, B * NV // 256, add, jnp.zeros((RL * NV, 128), F32))
    return out.reshape(RL, NV, 128)


def storage_level(part):
    section = lax.axis_index("lvl")
    return jnp.where(section < LV // 2, part, LV - 1 - part)


def relay_kernel(owned_hbm, columns_hbm, owner_hbm, sent_hbm, s_ref,
                 table, turn, owned_ref, columns_ref, owner_ref, sent_rows, sems):
    arrivals = [
        pltpu.make_async_copy(owned_hbm, owned_ref, sems.at[0]),
        pltpu.make_async_copy(columns_hbm, columns_ref, sems.at[1]),
        pltpu.make_async_copy(owner_hbm, owner_ref, sems.at[2]),
    ]
    for copy in arrivals:
        copy.start()
    for copy in arrivals:
        copy.wait()
    for group in range(ROWS // 8):
        base = group % 2 * 8
        for chunk in range(B * NV // 128):
            turn[group, pl.ds(chunk * 8, 8), :] = owned_ref[group // 2, base:base + 8, chunk * 128:(chunk + 1) * 128]
        for row in range(8):
            sent_rows[group * 8 + row] = turn[group, pl.ds(row, B * NV // 128, stride=8), :]
    sent_copy = pltpu.make_async_copy(sent_rows, sent_hbm, sems.at[3])
    sent_copy.start()
    cells = lax.axis_size("cell")
    span = RL * cells
    local = lax.broadcasted_iota(jnp.int32, columns_ref.shape, 2)
    offset = columns_ref[...] - local - lax.axis_index("cell") * RL
    offset = jnp.where(offset > span // 2, offset - span, offset)
    offset = jnp.where(offset < -(span // 2), offset + span, offset)
    place = jnp.clip(offset + local + W, 0, EXT - 1)
    for k in range(K):
        table[pl.ds(k * LV, LV), pl.ds(0, RL)] = place[k]
    owner = owner_ref[...]
    owner_row = owner % span
    owner_local = owner // span % LV * RL + owner_row % RL
    table[pl.ds(K * LV, LV), pl.ds(0, RL)] = owner_local // cells * cells + owner_row // RL
    table_copy = pltpu.make_async_copy(table, s_ref, sems.at[4])
    table_copy.start()
    table_copy.wait()
    sent_copy.wait()


def blocks_kernel(part, lower_hbm, dinv_hbm, rhs_hbm, w_ref, r_ref,
                  low, din, tiles, both, sems, wide_hi, wide_lo, rhs_ref, lines):
    level = storage_level(part)
    rhs_copy = pltpu.make_async_copy(rhs_hbm.at[level], rhs_ref, sems.at[2])
    copies = (
        pltpu.make_async_copy(lower_hbm.at[level], low, sems.at[0]),
        pltpu.make_async_copy(dinv_hbm.at[level], din, sems.at[1]),
    )
    for copy in (rhs_copy, *copies):
        copy.start()
    rhs_copy.wait()

    for half in range(2):
        for chunk in range(B * NV // 128):
            lines[half, pl.ds(chunk * 8, 8), :] = rhs_ref[half * 8:half * 8 + 8, chunk * 128:(chunk + 1) * 128]

    def load_rhs(row):
        return lines[row // 8, pl.ds(row % 8, B * NV // 128, stride=8), :]

    r_ref[...] = state_of_rows(load_rhs, wide_hi, wide_lo)
    left = low_half((B // 2, 128))
    left_wide = low_half((B, 128))
    for copy in copies:
        copy.wait()
    def turn_half(half, carry):
        start = pl.multiple_of(half * 8, 8)
        for k in range(K + 1):
            for chunk in range(B * B // 128):
                lanes = pl.ds(chunk * 128, 128)
                value = low[k, pl.ds(start, 8), lanes] if k < K else din[pl.ds(start, 8), lanes]
                tiles[half, k, pl.ds(chunk * 8, 8), :] = value
        return carry

    lax.fori_loop(0, 2, turn_half, 0)

    def row_blocks(half, row, slot):
        piece = [tiles[half, k, pl.ds(row, B // 2, stride=8), :] for k in range(K + 1)]
        turned = [other_half(p) for p in piece]
        both[slot, 0, pl.ds(0, B // 2, stride=2), :] = jnp.where(left, piece[0], turned[1])
        both[slot, 0, pl.ds(1, B // 2, stride=2), :] = jnp.where(left, turned[0], piece[1])
        both[slot, 1, pl.ds(0, B // 2, stride=2), :] = jnp.where(left, piece[2], turned[3])
        both[slot, 1, pl.ds(1, B // 2, stride=2), :] = jnp.where(left, turned[2], piece[3])
        first_tile, second = both[slot, 0], both[slot, 1]
        diag = other_half(second)[:, :B]
        diag_hi, diag_lo = split(diag)
        right_hi, right_lo = split(jnp.concatenate([first_tile, second], axis=1))
        top = nn(jnp.concatenate([diag_hi, diag_lo], axis=0), right_hi)
        product = top[:B] + top[B:] + nn(diag_hi, right_lo)
        tail = jnp.where(left_wide, product[:, 128:], second)
        hi, lo = split(jnp.concatenate([product[:, :128], tail], axis=1))
        w_ref[half * 8 + row] = jnp.concatenate([hi, lo], axis=0)

    def two_rows(pair, carry):
        for row in range(2):
            row_blocks(pair // 4, pair % 4 * 2 + row, row)
        return carry

    lax.fori_loop(0, RL // 2, two_rows, 0)


def adjoint_kernel(parts, s_ref, relayed_ref, *refs):
    *outs, wide_hi, wide_lo = refs
    for part, a_ref in zip(parts, outs):
        level = storage_level(part)

        def load(row):
            return relayed_ref[s_ref[K * LV + level, row]]

        a_ref[...] = state_of_rows(load, wide_hi, wide_lo)


def pack(x):
    half = x.shape[0] // 2
    return jnp.where(low_half((half, NV, 128)), x[:half], x[half:])


def unpack(x):
    turned = other_half(x)
    left = low_half(x.shape)
    return jnp.concatenate([jnp.where(left, x, turned), jnp.where(left, turned, x)], axis=0)


def is_even():
    return lax.axis_index("cell") % 2 == 0


def by_side(near, far, do):
    even = is_even()
    pl.when(even)(lambda: do(far, near))
    pl.when(jnp.logical_not(even))(lambda: do(near, far))


def in_eights(count, do):
    def eight(i, carry):
        for j in range(8):
            do(i, j)
        return carry

    lax.fori_loop(0, count // 8, eight, 0)


def forward_row(block, source, places, lookup, ghost=False):
    half = low_half((NV, 128))
    last = jnp.zeros_like(source) if ghost else -source
    if places is None:
        lhs = jnp.concatenate([jnp.zeros_like(source), jnp.where(half, 0.0, last)], axis=1)
    else:
        x0, x1, x2 = [lookup[i] for i in places]
        lhs = jnp.concatenate([jnp.where(half, x0, x1), jnp.where(half, x2, last)], axis=1)
    hi, lo = split(lhs)
    out = nt(jnp.concatenate([hi, lo], axis=0), block)
    out = out[:NV] + out[NV:]
    out = out + other_half(out)
    return source - out if ghost else -out


def clear(accs, window):
    for acc in accs:
        acc[pl.ds(0, window)] = jnp.zeros((window, NV, 128), F32)


def backward_row(block, value, places, accs):
    hi, lo = split(value)
    out = nn(jnp.concatenate([hi, lo], axis=0), block)
    out = out[:NV] + out[NV:]
    accs[0][places[0]] += out[:, :128]
    accs[1][places[1]] += out[:, :128]
    accs[2][places[2]] += out[:, 128:]
    return out[:, 128:]


def collected(accs, window):
    acc0, acc1, acc2 = [acc[pl.ds(0, window)] for acc in accs]
    total = jnp.where(low_half((window, NV, 128)), acc0 + acc2, acc1)
    return total + other_half(total)


def step_kernel(step, s_ref, w_ref, r_ref, a_ref, own_ref, near_ref, far_ref, res_ref, *refs):
    *outs, ext, acc0, acc1, acc2 = refs
    section = lax.axis_index("lvl")
    rnd, t = divmod(step, LV)
    first, handed = step == 0, t == 0

    def incoming(do):
        if handed:
            do(near_ref, far_ref)
        else:
            by_side(near_ref, far_ref, do)

    def outgoing(to_left, to_right, own):
        def put(near, far):
            if len(outs) == 1:
                outs[0][0] = near
                outs[0][1] = far
            else:
                outs[1][...] = near
                outs[2][...] = far

        if len(outs) == 3:
            outs[0][...] = own
        if len(outs) == 3 and t == LV - 1:
            put(to_left, to_right)
        else:
            even = is_even()
            pl.when(even)(lambda: put(to_right, to_left))
            pl.when(jnp.logical_not(even))(lambda: put(to_left, to_right))

    @pl.when(section == rnd)
    def _():
        if not first:
            ext[pl.ds(W, RL)] = unpack(own_ref[...])

            def fill(from_left, from_right):
                ext[pl.ds(0, W)] = unpack(from_left[...])
                ext[pl.ds(W + RL, W)] = unpack(from_right[...])

            incoming(fill)

        def one(i, j):
            q = i * 8 + j
            places = None if first else [s_ref[k * LV + t, q] for k in range(K)]
            res_ref[q] = forward_row(w_ref[q], r_ref[q], places, ext)

        in_eights(RL, one)
        x = res_ref[...]
        if len(outs) == 1:
            outgoing(pack(x), pack(x), None)
        else:
            outgoing(pack(x[:W]), pack(x[W:]), pack(x))

    @pl.when(section == LV - 1 - rnd)
    def _():
        level = LV - 1 - t
        if not first:
            ext[pl.ds(0, RL)] = unpack(own_ref[...])

            def add(from_left, from_right):
                ext[pl.ds(0, W)] += unpack(from_left[...])
                ext[pl.ds(W, W)] += unpack(from_right[...])

            incoming(add)
        accs = (acc0, acc1, acc2)
        clear(accs, EXT)

        def one(i, j):
            q = i * 8 + j
            value = a_ref[q] if first else a_ref[q] - ext[q]
            res_ref[q] = backward_row(w_ref[q], value, [s_ref[k * LV + level, q] for k in range(K)], accs)

        in_eights(RL, one)
        total = collected(accs, EXT)
        if len(outs) == 1:
            outgoing(pack(total[:RL]), pack(total[RL:]), None)
        else:
            outgoing(pack(total[:W]), pack(total[W + RL:]), pack(total[W:W + RL]))


def pair_kernel(rnd, t, s_ref, ghost_s, w0_ref, w1_ref, r0_ref, r1_ref, a0_ref, a1_ref, g_ref, gs_ref,
                own_near, own_far, near_ref, far_ref, res0_ref, res1_ref, *refs):
    *outs, ext, ext2, acc0, acc1, acc2 = refs
    section = lax.axis_index("lvl")

    def outgoing(to_left, to_right):
        def put(near, far):
            if len(outs) == 1:
                outs[0][0] = near
                outs[0][1] = far
            else:
                outs[0][...] = near
                outs[1][...] = far

        even = is_even()
        pl.when(even)(lambda: put(to_right, to_left))
        pl.when(jnp.logical_not(even))(lambda: put(to_left, to_right))

    def own_places(level, q, shift):
        return [s_ref[k * LV + level, q] + shift for k in range(K)]

    def ghost_places(ghost):
        return [ghost_s[k, ghost] for k in range(K)]

    @pl.when(section == rnd)
    def _():
        ext[pl.ds(RL, RL)] = unpack(own_near[...])

        def fill(from_left, from_right):
            ext[pl.ds(0, RL)] = unpack(from_left[...])
            ext[pl.ds(2 * RL, RL)] = unpack(from_right[...])

        by_side(near_ref, far_ref, fill)

        def ghost_row(i, j):
            ghost = i * 8 + j
            ext2[i * (W + RL) + j] = forward_row(g_ref[ghost], gs_ref[ghost], ghost_places(ghost), ext, True)

        def first_row(i, j):
            q = i * 8 + j
            x = forward_row(w0_ref[q], r0_ref[q], own_places(t, q, W), ext)
            ext2[W + q] = x
            res0_ref[q] = x

        def second_row(i, j):
            q = i * 8 + j
            res1_ref[q] = forward_row(w1_ref[q], r1_ref[q], own_places(t + 1, q, 0), ext2)

        in_eights(2 * W, ghost_row)
        in_eights(RL, first_row)
        in_eights(RL, second_row)
        x = res1_ref[...]
        outgoing(pack(x), pack(x))

    @pl.when(section == LV - 1 - rnd)
    def _():
        level = LV - 1 - t

        def gather(own_left, own_right):
            ext[pl.ds(0, RL)] = unpack(own_left[...])
            ext[pl.ds(RL, RL)] = unpack(own_right[...])

        def add(from_left, from_right):
            ext[pl.ds(0, RL)] += unpack(from_left[...])
            ext[pl.ds(RL, RL)] += unpack(from_right[...])

        by_side(own_near, own_far, gather)
        by_side(near_ref, far_ref, add)
        accs = (acc0, acc1, acc2)
        clear(accs, EXT + RL)

        def ghost_row(i, j):
            ghost = i * 8 + j
            backward_row(g_ref[ghost], gs_ref[ghost] - ext[i * (W + RL) + j], ghost_places(ghost), accs)

        def first_row(i, j):
            q = i * 8 + j
            res0_ref[q] = backward_row(w0_ref[q], a0_ref[q] - ext[W + q], own_places(level, q, W), accs)

        in_eights(2 * W, ghost_row)
        in_eights(RL, first_row)
        ext2[pl.ds(0, RL)] = collected(accs, EXT + RL)[RL:2 * RL]
        clear(accs, EXT)

        def second_row(i, j):
            q = i * 8 + j
            res1_ref[q] = backward_row(w1_ref[q], a1_ref[q] - ext2[q], own_places(level - 1, q, 0), accs)

        in_eights(RL, second_row)
        total = collected(accs, EXT)
        outgoing(pack(total[:RL]), pack(total[RL:]))


def ghost_send_kernel(part, s_ref, w_ref, r_ref, a_ref, near_ref, far_ref):
    forward = lax.axis_index("lvl") >= LV // 2
    shift = jnp.where(is_even(), W, 0)
    sub = lax.broadcasted_iota(jnp.int32, (8, 128), 0)
    left = low_half((B // 2, 128))
    left8 = low_half((8, 128))
    level = storage_level(part)
    for out_ref, base in ((near_ref, shift), (far_ref, W - shift)):

        def one(i, carry):
            block = w_ref[base + i]
            block = block[:B].astype(F32) + block[B:].astype(F32)
            out_ref[i, pl.ds(0, B), :] = block[:, :128]
            third = block[:, 128:]
            out_ref[i, pl.ds(B, B // 2), :] = jnp.where(left, third[:B // 2], other_half(third[B // 2:]))
            direct = forward_row(w_ref[base + i], r_ref[base + i], None, None)
            value = jnp.where(forward, direct, a_ref[base + i])
            out_ref[i, pl.ds(96, 8), :] = jnp.where(left8, value[:8], value[8:])
            places = jnp.zeros((8, 128), F32)
            for k in range(K):
                place = s_ref[k * LV + level, base + i].astype(F32)
                places = jnp.where(sub == k, place, places)
            out_ref[i, pl.ds(104, 8), :] = places
            return carry

        lax.fori_loop(0, W, one, 0, unroll=2)


def ghost_receive_kernel(near_ref, far_ref, g_ref, gs_ref, t_ref, table, sem):
    shift = jnp.where(is_even(), W, 0)
    lane = lax.broadcasted_iota(jnp.int32, (8, 128), 1)
    left = low_half((B // 2, 128))
    places = jnp.zeros((8, 128), F32)
    for in_ref, base in ((near_ref, shift), (far_ref, W - shift)):

        def one(i, places):
            first = in_ref[i, pl.ds(0, B), :]
            packed = in_ref[i, pl.ds(B, B // 2), :]
            third = jnp.concatenate(
                [jnp.where(left, packed, 0.0), jnp.where(left, other_half(packed), 0.0)], axis=0)
            hi, lo = split(jnp.concatenate([first, third], axis=1))
            g_ref[base + i] = jnp.concatenate([hi, lo], axis=0)
            gs_ref[base + i] = unpack(in_ref[i, pl.ds(96, 8), :].reshape(1, 8, 128)).reshape(NV, 128)
            return jnp.where(lane == base + i, in_ref[i, pl.ds(104, 8), :], places)

        places = lax.fori_loop(0, W, one, places, unroll=2)
    places = places.astype(jnp.int32) + jnp.where(lane < W, -W, RL + W)
    table[pl.ds(0, 8), :] = jnp.clip(places, 0, EXT + RL - 1)
    table[pl.ds(8, 8), :] = jnp.zeros((8, 128), jnp.int32)
    copy = pltpu.make_async_copy(table, t_ref, sem)
    copy.start()
    copy.wait()


def rows_kernel(rnd, levels, *refs):
    *refs, sol_ref, adj_ref, spread_ref, lines = refs
    results = refs[:len(levels)]
    section = lax.axis_index("lvl")
    forward = section == rnd

    @pl.when(jnp.logical_or(forward, section == LV - 1 - rnd))
    def _():
        spread = jnp.where(low_half((B * NV, 128)), 0.0, spread_matrix().astype(F32)).astype(BF16)
        spread_ref[...] = spread.reshape(B * NV // 128, 128, 128)
        mask = own_lane(RL * NV)
        for t, x in zip(levels, results):
            hi, lo = split(x[...].reshape(RL * NV, 128))

            def one(chunk, carry):
                part = spread_ref[chunk]
                wide = jnp.where(mask, nt(hi, part) + nt(lo, part), 0.0)
                lines[chunk] = jnp.sum(wide.reshape(RL, NV, 128), axis=1)
                return carry

            lax.fori_loop(0, B * NV // 128, one, 0, unroll=8 if rnd == LV - 1 and levels[0] else 1)
            for chunk in range(B * NV // 128):
                lanes = pl.ds(chunk * 128, 128)

                @pl.when(forward)
                def _():
                    sol_ref[t, :, lanes] = lines[chunk]

                @pl.when(jnp.logical_not(forward))
                def _():
                    adj_ref[LV - 1 - t, :, lanes] = lines[chunk]


def vspec():
    return pl.BlockSpec(memory_space=VMEM)


def sspec():
    return pl.BlockSpec(memory_space=SMEM)


def hspec():
    return pl.BlockSpec(memory_space=pl.ANY)


STATE = (RL, NV, 128)
OWN = (RL // 2, NV, 128)
SIDE = (W // 2, NV, 128)
MSGS = (2, RL // 2, NV, 128)
GHOST = (W, 112, 128)
GHOST_STEPS = {1: 3, 2: 1}
TABLE = ((K + 1) * LV, 128)
BLOCKS = (RL, 2 * B, 256)
SMEM_TABLE = SMEM(TABLE, jnp.int32)
OUT = (LV, RL, B * NV)


def params(mib):
    return pltpu.CompilerParams(vmem_limit_bytes=mib * MIB)


def cost(us):
    return pl.CostEstimate(flops=int(us * 1e9), bytes_accessed=int(us * 3e6), transcendentals=0)


def relay(owned, columns, owner):
    sent = (ROWS, B * NV // 128, 128)
    return pl.pallas_call(
        relay_kernel,
        out_shape=(pltpu.HBM(sent, F32), SMEM_TABLE),
        in_specs=[hspec()] * 3,
        out_specs=(hspec(), sspec()),
        scratch_shapes=[
            VMEM(TABLE, jnp.int32),
            VMEM((ROWS // 8, B * NV // 16, 128), F32),
            VMEM(owned.shape, F32),
            VMEM(columns.shape, jnp.int32),
            VMEM(owner.shape, jnp.int32),
            VMEM(sent, F32),
            pltpu.SemaphoreType.DMA((5,)),
        ],
        compiler_params=params(8),
        cost_estimate=cost(2.0),
        name="relay",
    )(in_hbm(owned), in_hbm(columns), in_hbm(owner))


def prepare(part, lower, dinv, rhs):
    wide = VMEM((RL * NV, B * NV), BF16)
    scratch = [
        VMEM((K, RL, B * B), F32),
        VMEM((RL, B * B), F32),
        VMEM((2, K + 1, 8 * B * B // 128, 128), F32),
        VMEM((4, 2, B, 128), F32),
        pltpu.SemaphoreType.DMA((3,)),
        wide,
        wide,
        VMEM((RL, B * NV), F32),
        VMEM((2, B * NV // 16, 128), F32),
    ]
    shapes = [VMEM(BLOCKS, BF16), VMEM(STATE, F32)]
    specs = [hspec(), hspec(), hspec()]
    return pl.pallas_call(
        partial(blocks_kernel, part),
        out_shape=shapes,
        in_specs=specs,
        out_specs=[vspec()] * len(shapes),
        scratch_shapes=scratch,
        compiler_params=params(12),
        cost_estimate=cost(2.5),
        name="prepare%d" % part,
    )(in_hbm(lower), in_hbm(dinv), in_hbm(rhs))


def adjoint_state(parts, table, relayed):
    wide = VMEM((RL * NV, B * NV), BF16)
    return call(partial(adjoint_kernel, parts), "adjoint_state", 0.6 * len(parts), [table, relayed],
                [VMEM(STATE, F32)] * len(parts), [wide, wide])


def call(body, name, us, kernel_args, shapes, scratch=(), mib=8, **more):
    def place(x):
        return in_smem(x) if x.dtype == jnp.int32 and x.shape == TABLE else in_vmem(x)

    def spec(x):
        return sspec() if x.dtype == jnp.int32 and x.shape == TABLE else vspec()

    return pl.pallas_call(
        body,
        out_shape=tuple(shapes),
        in_specs=[spec(x) for x in kernel_args],
        out_specs=tuple(sspec() if isinstance(x, type(SMEM_TABLE)) and x.memory_space == SMEM else vspec() for x in shapes),
        scratch_shapes=list(scratch),
        compiler_params=params(mib),
        cost_estimate=cost(us),
        name=name,
        **more,
    )(*[place(x) for x in kernel_args])


def run_step(step, table, blocks, source, adjoint, own, near, far):
    kernel_args = [table, blocks, source, adjoint]
    if own is not None:
        kernel_args += [own, near, far]

    def body(*refs):
        head, refs = refs[:4], refs[4:]
        arrivals = [None] * 3
        if own is not None:
            arrivals, refs = refs[:3], refs[3:]
        step_kernel(step, *head, *arrivals, *refs)

    shapes = [VMEM(STATE, F32)]
    shapes += [VMEM(MSGS, F32)] if step == 2 * LV - 1 else [VMEM(OWN, F32), VMEM(SIDE, F32), VMEM(SIDE, F32)]
    return call(body, "step%d" % step, 0.6, kernel_args, shapes, [VMEM((EXT, NV, 128), F32)] * 4)


def run_pair(rnd, t, table, blocks, source, adjoint, ghost, arrivals):
    kernel_args = [table, ghost[-1], *blocks, *source, *adjoint, *ghost[:-1], *arrivals]
    shapes = [VMEM(STATE, F32)] * 2
    shapes += [VMEM(OWN, F32)] * 2 if t == 0 else [VMEM(MSGS, F32)]

    scratch = [VMEM((EXT + RL, NV, 128), F32), VMEM((EXT, NV, 128), F32)] + [VMEM((EXT + RL, NV, 128), F32)] * 3
    return call(partial(pair_kernel, rnd, t), "pair%d_%d" % (rnd, t), 1.8, kernel_args, shapes, scratch)


def ghost_send(part, table, blocks, source, adjoint):
    return call(partial(ghost_send_kernel, part), "ghost_send", 0.5,
                [table, blocks, source, adjoint], [VMEM(GHOST, F32)] * 2)


def ghost_receive(near, far):
    return call(ghost_receive_kernel, "ghost_receive", 0.5, [near, far],
                [VMEM(BLOCKS, BF16), VMEM(STATE, F32), SMEM_TABLE],
                [VMEM(TABLE, jnp.int32), pltpu.SemaphoreType.DMA])


def to_rows(rnd, levels, results, outs):
    outs = [] if outs is None else list(outs)
    place = len(results)
    return call(partial(rows_kernel, rnd, levels), "rows%d_%d" % (rnd, levels[0]), 0.6 * len(levels),
                [*results, *outs], [VMEM(OUT, F32)] * 2,
                [VMEM((B * NV // 128, 128, 128), BF16), VMEM((B * NV // 128, RL, 128), F32)],
                input_output_aliases={place: 0, place + 1: 1} if outs else {})


def after(values, done):
    return lax.optimization_barrier((values, done))[0]


def per_device(rhs, adjoint_owned, owner_of, columns, lower, dinv):
    cells = lax.axis_size("cell")
    sections = lax.axis_size("lvl")
    lower = jnp.transpose(lower, (0, 2, 1, 3))
    columns = jnp.transpose(columns, (2, 0, 1))
    blocks, source, adjoint = ([None] * LV for _ in range(3))
    sent, table = relay(adjoint_owned, columns, owner_of)
    relayed = lax.all_to_all(sent.reshape(1, cells, B * NV), "cell", split_axis=1, concat_axis=1, tiled=True)
    relayed = relayed.reshape(ROWS, B * NV // 128, 128)
    for part in range(LV):
        blocks[part], source[part] = prepare(part, *after((lower, dinv, rhs), sent))
    adjoint[0], = adjoint_state((0,), table, relayed)

    near_of = [i ^ 1 for i in range(cells)]
    far_of = [(i + 1 if i % 2 else i - 1) % cells for i in range(cells)]

    def exchange(near, far):
        far_in = lax.ppermute(far, "cell", list(enumerate(far_of)))
        near_in = lax.ppermute(near, "cell", list(enumerate(near_of)))
        return near_in, far_in

    def shift_handoff(x, by):
        moves = [(0, 1), (sections - 1, sections - 2)]
        pairs = [(a * cells + i, b * cells + (i + by) % cells) for a, b in moves for i in range(cells)]
        return lax.ppermute(x, ("lvl", "cell"), pairs)

    def handoff(msgs, rnd):
        partner = [1, 0, 3, 2] if rnd % 2 == 0 else [3, 2, 1, 0]
        pairs = [(s * cells + i, partner[s] * cells + i) for s in range(sections) for i in range(cells)]
        return lax.ppermute(msgs, ("lvl", "cell"), pairs)

    ghosts = {}
    own = near = far = outs = None
    for step in range(2 * LV):
        rnd, t = divmod(step, LV)
        result, *sent_out = run_step(step, table, blocks[t], source[t], adjoint[t], own, near, far)
        if step == 0:
            adjoint[1:] = adjoint_state((1, 2, 3), table, after(relayed, sent_out[-1]))
        if step in GHOST_STEPS:
            part = GHOST_STEPS[step]
            shared = after((blocks[part], source[part], adjoint[part]), sent_out[-1])
            ghosts[part] = ghost_receive(*exchange(*ghost_send(part, table, *shared)))
        if t < LV - 1:
            own = sent_out[0]
            near, far = exchange(*sent_out[1:])
        elif rnd == 0:
            own, to_left, to_right = sent_out
            own, near, far = shift_handoff(own, 0), shift_handoff(to_right, 1), shift_handoff(to_left, -1)
        results = [result] if t == 0 else [*results, result]
        if t == LV - 1:
            outs = to_rows(rnd, tuple(range(LV)), results, outs)
    msgs = sent_out[0]
    for rnd in range(LV // 2, sections):
        msgs = handoff(msgs, rnd - 1)
        own_near, own_far = msgs[0], msgs[1]
        for t in (0, 2):
            parts = (LV - 1 - t, LV - 2 - t)
            arrivals = (own_near, own_far, *exchange(own_near, own_far))
            picked = [[x[p] for p in parts] for x in (blocks, source, adjoint)]
            first, second, *sent_out = run_pair(rnd, t, table, *picked, ghosts[parts[0]], arrivals)
            if t == 0:
                own_near, own_far = sent_out
            outs = to_rows(rnd, (t, t + 1), (first, second), outs)
        msgs = sent_out[0]
    return outs


def solution(mesh):
    return jax.shard_map(
        per_device,
        mesh=mesh,
        in_specs=(
            P("lvl", "cell", None),
            P("lvl", "cell", None),
            P("lvl", "cell"),
            P("lvl", "cell", None),
            P("lvl", "cell", None, None),
            P("lvl", "cell", None),
        ),
        out_specs=(P("lvl", "cell", None), P("lvl", "cell", None)),
        check_vma=False,
    )
```

```python
from functools import partial

import jax
import jax.numpy as jnp
from jax import lax
from jax.experimental import pallas as pl
from jax.experimental.pallas import tpu as pltpu
from jax.sharding import PartitionSpec as P

B = 64
NV = 16
K = 3
W = 8
LV = 4
RL = 16
ROWS = LV * RL
EXT = RL + 2 * W
VMEM = pltpu.VMEM
SMEM = pltpu.SMEM
F32 = jnp.float32
BF16 = jnp.bfloat16
MIB = 1 << 20


def in_vmem(x):
    return pltpu.with_memory_space_constraint(x, VMEM)


def in_hbm(x):
    return pltpu.with_memory_space_constraint(x, pltpu.HBM)


def in_smem(x):
    return pltpu.with_memory_space_constraint(x, SMEM)


def split(x):
    hi = x.astype(BF16)
    lo = (x - hi.astype(F32)).astype(BF16)
    return hi, lo


def nn(a, b):
    return jnp.dot(a, b, preferred_element_type=F32)


def nt(a, b):
    return lax.dot_general(a, b, (((1,), (1,)), ((), ())), preferred_element_type=F32)


def low_half(shape):
    return lax.broadcasted_iota(jnp.int32, shape, len(shape) - 1) % 128 < B


def other_half(x):
    return pltpu.roll(x, B, axis=x.ndim - 1)


def spread_matrix():
    row = lax.broadcasted_iota(jnp.int32, (B * NV, 128), 0) // NV
    col = lax.broadcasted_iota(jnp.int32, (B * NV, 128), 1) % B
    return jnp.where(row == col, 1.0, 0.0).astype(BF16)


def own_lane(rows):
    lane = lax.broadcasted_iota(jnp.int32, (rows, 128), 1) % NV
    vec = lax.broadcasted_iota(jnp.int32, (rows, 128), 0) % NV
    return lane == vec


def state_of_rows(load, wide_hi, wide_lo):
    mask = own_lane(NV)

    def one(row, carry):
        block = load(row)
        for chunk in range(B * NV // 128):
            value = jnp.broadcast_to(block[chunk:chunk + 1], (NV, 128))
            hi, lo = split(jnp.where(mask, value, 0.0))
            place = (pl.ds(pl.multiple_of(row * NV, NV), NV), pl.ds(chunk * 128, 128))
            wide_hi[place] = hi
            wide_lo[place] = lo
        return carry

    lax.fori_loop(0, RL, one, 0, unroll=2)
    row = lax.broadcasted_iota(jnp.int32, (256, 128), 0) // NV
    col = lax.broadcasted_iota(jnp.int32, (256, 128), 1) % B

    def add(part, total):
        spread = jnp.where(row + part * (256 // NV) == col, 1.0, 0.0).astype(BF16)
        lanes = pl.ds(pl.multiple_of(part * 256, 256), 256)
        return total + nn(wide_hi[:, lanes], spread) + nn(wide_lo[:, lanes], spread)

    out = lax.fori_loop(0, B * NV // 256, add, jnp.zeros((RL * NV, 128), F32))
    return out.reshape(RL, NV, 128)


def storage_level(part):
    section = lax.axis_index("lvl")
    return jnp.where(section < LV // 2, part, LV - 1 - part)


def relay_kernel(owned_hbm, columns_hbm, owner_hbm, sent_hbm, s_ref,
                 table, turn, owned_ref, columns_ref, owner_ref, sent_rows, sems):
    arrivals = [
        pltpu.make_async_copy(owned_hbm, owned_ref, sems.at[0]),
        pltpu.make_async_copy(columns_hbm, columns_ref, sems.at[1]),
        pltpu.make_async_copy(owner_hbm, owner_ref, sems.at[2]),
    ]
    for copy in arrivals:
        copy.start()
    for copy in arrivals:
        copy.wait()
    for group in range(ROWS // 8):
        base = group % 2 * 8
        for chunk in range(B * NV // 128):
            turn[group, pl.ds(chunk * 8, 8), :] = owned_ref[group // 2, base:base + 8, chunk * 128:(chunk + 1) * 128]
        for row in range(8):
            sent_rows[group * 8 + row] = turn[group, pl.ds(row, B * NV // 128, stride=8), :]
    sent_copy = pltpu.make_async_copy(sent_rows, sent_hbm, sems.at[3])
    sent_copy.start()
    cells = lax.axis_size("cell")
    span = RL * cells
    local = lax.broadcasted_iota(jnp.int32, columns_ref.shape, 2)
    offset = columns_ref[...] - local - lax.axis_index("cell") * RL
    offset = jnp.where(offset > span // 2, offset - span, offset)
    offset = jnp.where(offset < -(span // 2), offset + span, offset)
    place = jnp.clip(offset + local + W, 0, EXT - 1)
    for k in range(K):
        table[pl.ds(k * LV, LV), pl.ds(0, RL)] = place[k]
    owner = owner_ref[...]
    owner_row = owner % span
    owner_local = owner // span % LV * RL + owner_row % RL
    table[pl.ds(K * LV, LV), pl.ds(0, RL)] = owner_local // cells * cells + owner_row // RL
    table_copy = pltpu.make_async_copy(table, s_ref, sems.at[4])
    table_copy.start()
    table_copy.wait()
    sent_copy.wait()


def blocks_kernel(part, lower_hbm, dinv_hbm, rhs_hbm, w_ref, r_ref,
                  low, din, tiles, both, sems, wide_hi, wide_lo, rhs_ref, lines):
    level = storage_level(part)
    rhs_copy = pltpu.make_async_copy(rhs_hbm.at[level], rhs_ref, sems.at[2])
    copies = (
        pltpu.make_async_copy(lower_hbm.at[level], low, sems.at[0]),
        pltpu.make_async_copy(dinv_hbm.at[level], din, sems.at[1]),
    )
    for copy in (rhs_copy, *copies):
        copy.start()
    rhs_copy.wait()

    for half in range(2):
        for chunk in range(B * NV // 128):
            lines[half, pl.ds(chunk * 8, 8), :] = rhs_ref[half * 8:half * 8 + 8, chunk * 128:(chunk + 1) * 128]

    def load_rhs(row):
        return lines[row // 8, pl.ds(row % 8, B * NV // 128, stride=8), :]

    r_ref[...] = state_of_rows(load_rhs, wide_hi, wide_lo)
    left = low_half((B // 2, 128))
    left_wide = low_half((B, 128))
    for copy in copies:
        copy.wait()
    def turn_half(half, carry):
        start = pl.multiple_of(half * 8, 8)
        for k in range(K + 1):
            for chunk in range(B * B // 128):
                lanes = pl.ds(chunk * 128, 128)
                value = low[k, pl.ds(start, 8), lanes] if k < K else din[pl.ds(start, 8), lanes]
                tiles[half, k, pl.ds(chunk * 8, 8), :] = value
        return carry

    lax.fori_loop(0, 2, turn_half, 0)

    def row_blocks(half, row, slot):
        piece = [tiles[half, k, pl.ds(row, B // 2, stride=8), :] for k in range(K + 1)]
        turned = [other_half(p) for p in piece]
        both[slot, 0, pl.ds(0, B // 2, stride=2), :] = jnp.where(left, piece[0], turned[1])
        both[slot, 0, pl.ds(1, B // 2, stride=2), :] = jnp.where(left, turned[0], piece[1])
        both[slot, 1, pl.ds(0, B // 2, stride=2), :] = jnp.where(left, piece[2], turned[3])
        both[slot, 1, pl.ds(1, B // 2, stride=2), :] = jnp.where(left, turned[2], piece[3])
        first_tile, second = both[slot, 0], both[slot, 1]
        diag = other_half(second)[:, :B]
        diag_hi, diag_lo = split(diag)
        right_hi, right_lo = split(jnp.concatenate([first_tile, second], axis=1))
        top = nn(jnp.concatenate([diag_hi, diag_lo], axis=0), right_hi)
        product = top[:B] + top[B:] + nn(diag_hi, right_lo)
        tail = jnp.where(left_wide, product[:, 128:], second)
        hi, lo = split(jnp.concatenate([product[:, :128], tail], axis=1))
        w_ref[half * 8 + row] = jnp.concatenate([hi, lo], axis=0)

    def four_rows(pair, carry):
        for row in range(4):
            row_blocks(pair // 2, pair % 2 * 4 + row, row)
        return carry

    lax.fori_loop(0, RL // 4, four_rows, 0)


def adjoint_kernel(parts, s_ref, relayed_ref, *refs):
    *outs, wide_hi, wide_lo = refs
    for part, a_ref in zip(parts, outs):
        level = storage_level(part)

        def load(row):
            return relayed_ref[s_ref[K * LV + level, row]]

        a_ref[...] = state_of_rows(load, wide_hi, wide_lo)


def pack(x):
    half = x.shape[0] // 2
    return jnp.where(low_half((half, NV, 128)), x[:half], x[half:])


def unpack(x):
    turned = other_half(x)
    left = low_half(x.shape)
    return jnp.concatenate([jnp.where(left, x, turned), jnp.where(left, turned, x)], axis=0)


def is_even():
    return lax.axis_index("cell") % 2 == 0


def by_side(near, far, do):
    even = is_even()
    pl.when(even)(lambda: do(far, near))
    pl.when(jnp.logical_not(even))(lambda: do(near, far))


def in_eights(count, do):
    for i in range(count // 8):
        for j in range(8):
            do(i, j)


def forward_row(block, source, places, lookup, ghost=False):
    half = low_half((NV, 128))
    last = jnp.zeros_like(source) if ghost else -source
    if places is None:
        lhs = jnp.concatenate([jnp.zeros_like(source), jnp.where(half, 0.0, last)], axis=1)
    else:
        x0, x1, x2 = [lookup[i] for i in places]
        lhs = jnp.concatenate([jnp.where(half, x0, x1), jnp.where(half, x2, last)], axis=1)
    hi, lo = split(lhs)
    out = nt(jnp.concatenate([hi, lo], axis=0), block)
    out = out[:NV] + out[NV:]
    out = out + other_half(out)
    return source - out if ghost else -out


def clear(accs, window):
    for acc in accs:
        acc[pl.ds(0, window)] = jnp.zeros((window, NV, 128), F32)


def backward_row(block, value, places, accs):
    hi, lo = split(value)
    out = nn(jnp.concatenate([hi, lo], axis=0), block)
    out = out[:NV] + out[NV:]
    accs[0][places[0]] += out[:, :128]
    accs[1][places[1]] += out[:, :128]
    accs[2][places[2]] += out[:, 128:]
    return out[:, 128:]


def collected(accs, window):
    acc0, acc1, acc2 = [acc[pl.ds(0, window)] for acc in accs]
    total = jnp.where(low_half((window, NV, 128)), acc0 + acc2, acc1)
    return total + other_half(total)


def step_kernel(step, s_ref, w_ref, r_ref, a_ref, own_ref, near_ref, far_ref, res_ref, *refs):
    *outs, ext, acc0, acc1, acc2 = refs
    section = lax.axis_index("lvl")
    rnd, t = divmod(step, LV)
    first, handed = step == 0, t == 0

    def incoming(do):
        if handed:
            do(near_ref, far_ref)
        else:
            by_side(near_ref, far_ref, do)

    def outgoing(to_left, to_right, own):
        def put(near, far):
            if len(outs) == 1:
                outs[0][0] = near
                outs[0][1] = far
            else:
                outs[1][...] = near
                outs[2][...] = far

        if len(outs) == 3:
            outs[0][...] = own
        if len(outs) == 3 and t == LV - 1:
            put(to_left, to_right)
        else:
            even = is_even()
            pl.when(even)(lambda: put(to_right, to_left))
            pl.when(jnp.logical_not(even))(lambda: put(to_left, to_right))

    @pl.when(section == rnd)
    def _():
        if not first:
            ext[pl.ds(W, RL)] = unpack(own_ref[...])

            def fill(from_left, from_right):
                ext[pl.ds(0, W)] = unpack(from_left[...])
                ext[pl.ds(W + RL, W)] = unpack(from_right[...])

            incoming(fill)

        def one(i, j):
            q = i * 8 + j
            places = None if first else [s_ref[k * LV + t, q] for k in range(K)]
            res_ref[q] = forward_row(w_ref[q], r_ref[q], places, ext)

        in_eights(RL, one)
        x = res_ref[...]
        if len(outs) == 1:
            outgoing(pack(x), pack(x), None)
        else:
            outgoing(pack(x[:W]), pack(x[W:]), pack(x))

    @pl.when(section == LV - 1 - rnd)
    def _():
        level = LV - 1 - t
        if not first:
            ext[pl.ds(0, RL)] = unpack(own_ref[...])

            def add(from_left, from_right):
                ext[pl.ds(0, W)] += unpack(from_left[...])
                ext[pl.ds(W, W)] += unpack(from_right[...])

            incoming(add)
        accs = (acc0, acc1, acc2)
        clear(accs, EXT)

        def one(i, j):
            q = i * 8 + j
            value = a_ref[q] if first else a_ref[q] - ext[q]
            res_ref[q] = backward_row(w_ref[q], value, [s_ref[k * LV + level, q] for k in range(K)], accs)

        in_eights(RL, one)
        total = collected(accs, EXT)
        if len(outs) == 1:
            outgoing(pack(total[:RL]), pack(total[RL:]), None)
        else:
            outgoing(pack(total[:W]), pack(total[W + RL:]), pack(total[W:W + RL]))


def pair_kernel(rnd, t, s_ref, ghost_s, w0_ref, w1_ref, r0_ref, r1_ref, a0_ref, a1_ref, g_ref, gs_ref,
                own_near, own_far, near_ref, far_ref, res0_ref, res1_ref, *refs):
    *outs, ext, ext2, acc0, acc1, acc2 = refs
    section = lax.axis_index("lvl")

    def outgoing(to_left, to_right):
        def put(near, far):
            if len(outs) == 1:
                outs[0][0] = near
                outs[0][1] = far
            else:
                outs[0][...] = near
                outs[1][...] = far

        even = is_even()
        pl.when(even)(lambda: put(to_right, to_left))
        pl.when(jnp.logical_not(even))(lambda: put(to_left, to_right))

    def own_places(level, q, shift):
        return [s_ref[k * LV + level, q] + shift for k in range(K)]

    def ghost_places(ghost):
        return [ghost_s[k, ghost] for k in range(K)]

    @pl.when(section == rnd)
    def _():
        ext[pl.ds(RL, RL)] = unpack(own_near[...])

        def fill(from_left, from_right):
            ext[pl.ds(0, RL)] = unpack(from_left[...])
            ext[pl.ds(2 * RL, RL)] = unpack(from_right[...])

        by_side(near_ref, far_ref, fill)

        def ghost_row(i, j):
            ghost = i * 8 + j
            ext2[i * (W + RL) + j] = forward_row(g_ref[ghost], gs_ref[ghost], ghost_places(ghost), ext, True)

        def first_row(i, j):
            q = i * 8 + j
            x = forward_row(w0_ref[q], r0_ref[q], own_places(t, q, W), ext)
            ext2[W + q] = x
            res0_ref[q] = x

        def second_row(i, j):
            q = i * 8 + j
            res1_ref[q] = forward_row(w1_ref[q], r1_ref[q], own_places(t + 1, q, 0), ext2)

        in_eights(2 * W, ghost_row)
        in_eights(RL, first_row)
        in_eights(RL, second_row)
        x = res1_ref[...]
        outgoing(pack(x), pack(x))

    @pl.when(section == LV - 1 - rnd)
    def _():
        level = LV - 1 - t

        def gather(own_left, own_right):
            ext[pl.ds(0, RL)] = unpack(own_left[...])
            ext[pl.ds(RL, RL)] = unpack(own_right[...])

        def add(from_left, from_right):
            ext[pl.ds(0, RL)] += unpack(from_left[...])
            ext[pl.ds(RL, RL)] += unpack(from_right[...])

        by_side(own_near, own_far, gather)
        by_side(near_ref, far_ref, add)
        accs = (acc0, acc1, acc2)
        clear(accs, EXT + RL)

        def ghost_row(i, j):
            ghost = i * 8 + j
            backward_row(g_ref[ghost], gs_ref[ghost] - ext[i * (W + RL) + j], ghost_places(ghost), accs)

        def first_row(i, j):
            q = i * 8 + j
            res0_ref[q] = backward_row(w0_ref[q], a0_ref[q] - ext[W + q], own_places(level, q, W), accs)

        in_eights(2 * W, ghost_row)
        in_eights(RL, first_row)
        ext2[pl.ds(0, RL)] = collected(accs, EXT + RL)[RL:2 * RL]
        clear(accs, EXT)

        def second_row(i, j):
            q = i * 8 + j
            res1_ref[q] = backward_row(w1_ref[q], a1_ref[q] - ext2[q], own_places(level - 1, q, 0), accs)

        in_eights(RL, second_row)
        total = collected(accs, EXT)
        outgoing(pack(total[:RL]), pack(total[RL:]))


def ghost_send_kernel(part, s_ref, w_ref, r_ref, a_ref, near_ref, far_ref):
    forward = lax.axis_index("lvl") >= LV // 2
    shift = jnp.where(is_even(), W, 0)
    sub = lax.broadcasted_iota(jnp.int32, (8, 128), 0)
    left = low_half((B // 2, 128))
    left8 = low_half((8, 128))
    level = storage_level(part)
    for out_ref, base in ((near_ref, shift), (far_ref, W - shift)):

        def one(i, carry):
            block = w_ref[base + i]
            block = block[:B].astype(F32) + block[B:].astype(F32)
            out_ref[i, pl.ds(0, B), :] = block[:, :128]
            third = block[:, 128:]
            out_ref[i, pl.ds(B, B // 2), :] = jnp.where(left, third[:B // 2], other_half(third[B // 2:]))
            direct = forward_row(w_ref[base + i], r_ref[base + i], None, None)
            value = jnp.where(forward, direct, a_ref[base + i])
            out_ref[i, pl.ds(96, 8), :] = jnp.where(left8, value[:8], value[8:])
            places = jnp.zeros((8, 128), F32)
            for k in range(K):
                place = s_ref[k * LV + level, base + i].astype(F32)
                places = jnp.where(sub == k, place, places)
            out_ref[i, pl.ds(104, 8), :] = places
            return carry

        lax.fori_loop(0, W, one, 0)


def ghost_receive_kernel(near_ref, far_ref, g_ref, gs_ref, t_ref, table, sem):
    shift = jnp.where(is_even(), W, 0)
    lane = lax.broadcasted_iota(jnp.int32, (8, 128), 1)
    left = low_half((B // 2, 128))
    places = jnp.zeros((8, 128), F32)
    for in_ref, base in ((near_ref, shift), (far_ref, W - shift)):

        def one(i, places):
            first = in_ref[i, pl.ds(0, B), :]
            packed = in_ref[i, pl.ds(B, B // 2), :]
            third = jnp.concatenate(
                [jnp.where(left, packed, 0.0), jnp.where(left, other_half(packed), 0.0)], axis=0)
            hi, lo = split(jnp.concatenate([first, third], axis=1))
            g_ref[base + i] = jnp.concatenate([hi, lo], axis=0)
            gs_ref[base + i] = unpack(in_ref[i, pl.ds(96, 8), :].reshape(1, 8, 128)).reshape(NV, 128)
            return jnp.where(lane == base + i, in_ref[i, pl.ds(104, 8), :], places)

        places = lax.fori_loop(0, W, one, places)
    places = places.astype(jnp.int32) + jnp.where(lane < W, -W, RL + W)
    table[pl.ds(0, 8), :] = jnp.clip(places, 0, EXT + RL - 1)
    table[pl.ds(8, 8), :] = jnp.zeros((8, 128), jnp.int32)
    copy = pltpu.make_async_copy(table, t_ref, sem)
    copy.start()
    copy.wait()


def rows_kernel(rnd, levels, *refs):
    *refs, sol_ref, adj_ref, spread_ref = refs
    results = refs[:len(levels)]
    section = lax.axis_index("lvl")
    forward = section == rnd

    @pl.when(jnp.logical_or(forward, section == LV - 1 - rnd))
    def _():
        spread = jnp.where(low_half((B * NV, 128)), 0.0, spread_matrix().astype(F32)).astype(BF16)
        spread_ref[...] = spread.reshape(B * NV // 128, 128, 128)
        mask = own_lane(RL * NV)
        for t, x in zip(levels, results):
            hi, lo = split(x[...].reshape(RL * NV, 128))

            def one(chunk, carry):
                part = spread_ref[chunk]
                wide = jnp.where(mask, nt(hi, part) + nt(lo, part), 0.0)
                value = jnp.sum(wide.reshape(RL, NV, 128), axis=1)
                lanes = pl.ds(pl.multiple_of(chunk * 128, 128), 128)

                @pl.when(forward)
                def _():
                    sol_ref[t, :, lanes] = value

                @pl.when(jnp.logical_not(forward))
                def _():
                    adj_ref[LV - 1 - t, :, lanes] = value

                return carry

            lax.fori_loop(0, B * NV // 128, one, 0, unroll=4 if rnd == LV - 1 and levels[0] else 1)


def vspec():
    return pl.BlockSpec(memory_space=VMEM)


def sspec():
    return pl.BlockSpec(memory_space=SMEM)


def hspec():
    return pl.BlockSpec(memory_space=pl.ANY)


STATE = (RL, NV, 128)
OWN = (RL // 2, NV, 128)
SIDE = (W // 2, NV, 128)
MSGS = (2, RL // 2, NV, 128)
GHOST = (W, 112, 128)
GHOST_STEPS = {1: 3, 2: 1}
TABLE = ((K + 1) * LV, 128)
BLOCKS = (RL, 2 * B, 256)
SMEM_TABLE = SMEM(TABLE, jnp.int32)
OUT = (LV, RL, B * NV)


def params(mib):
    return pltpu.CompilerParams(vmem_limit_bytes=mib * MIB)


def cost(us):
    return pl.CostEstimate(flops=int(us * 1e9), bytes_accessed=int(us * 3e6), transcendentals=0)


def relay(owned, columns, owner):
    sent = (ROWS, B * NV // 128, 128)
    return pl.pallas_call(
        relay_kernel,
        out_shape=(pltpu.HBM(sent, F32), SMEM_TABLE),
        in_specs=[hspec()] * 3,
        out_specs=(hspec(), sspec()),
        scratch_shapes=[
            VMEM(TABLE, jnp.int32),
            VMEM((ROWS // 8, B * NV // 16, 128), F32),
            VMEM(owned.shape, F32),
            VMEM(columns.shape, jnp.int32),
            VMEM(owner.shape, jnp.int32),
            VMEM(sent, F32),
            pltpu.SemaphoreType.DMA((5,)),
        ],
        compiler_params=params(8),
        cost_estimate=cost(2.0),
        name="relay",
    )(in_hbm(owned), in_hbm(columns), in_hbm(owner))


def prepare(part, lower, dinv, rhs):
    wide = VMEM((RL * NV, B * NV), BF16)
    scratch = [
        VMEM((K, RL, B * B), F32),
        VMEM((RL, B * B), F32),
        VMEM((2, K + 1, 8 * B * B // 128, 128), F32),
        VMEM((4, 2, B, 128), F32),
        pltpu.SemaphoreType.DMA((3,)),
        wide,
        wide,
        VMEM((RL, B * NV), F32),
        VMEM((2, B * NV // 16, 128), F32),
    ]
    shapes = [VMEM(BLOCKS, BF16), VMEM(STATE, F32)]
    specs = [hspec(), hspec(), hspec()]
    return pl.pallas_call(
        partial(blocks_kernel, part),
        out_shape=shapes,
        in_specs=specs,
        out_specs=[vspec()] * len(shapes),
        scratch_shapes=scratch,
        compiler_params=params(12),
        cost_estimate=cost(2.5),
        name="prepare%d" % part,
    )(in_hbm(lower), in_hbm(dinv), in_hbm(rhs))


def adjoint_state(parts, table, relayed):
    wide = VMEM((RL * NV, B * NV), BF16)
    return call(partial(adjoint_kernel, parts), "adjoint_state", 0.6 * len(parts), [table, relayed],
                [VMEM(STATE, F32)] * len(parts), [wide, wide])


def call(body, name, us, kernel_args, shapes, scratch=(), mib=8, **more):
    def place(x):
        return in_smem(x) if x.dtype == jnp.int32 and x.shape == TABLE else in_vmem(x)

    def spec(x):
        return sspec() if x.dtype == jnp.int32 and x.shape == TABLE else vspec()

    return pl.pallas_call(
        body,
        out_shape=tuple(shapes),
        in_specs=[spec(x) for x in kernel_args],
        out_specs=tuple(sspec() if isinstance(x, type(SMEM_TABLE)) and x.memory_space == SMEM else vspec() for x in shapes),
        scratch_shapes=list(scratch),
        compiler_params=params(mib),
        cost_estimate=cost(us),
        name=name,
        **more,
    )(*[place(x) for x in kernel_args])


def run_step(step, table, blocks, source, adjoint, own, near, far):
    kernel_args = [table, blocks, source, adjoint]
    if own is not None:
        kernel_args += [own, near, far]

    def body(*refs):
        head, refs = refs[:4], refs[4:]
        arrivals = [None] * 3
        if own is not None:
            arrivals, refs = refs[:3], refs[3:]
        step_kernel(step, *head, *arrivals, *refs)

    shapes = [VMEM(STATE, F32)]
    shapes += [VMEM(MSGS, F32)] if step == 2 * LV - 1 else [VMEM(OWN, F32), VMEM(SIDE, F32), VMEM(SIDE, F32)]
    return call(body, "step%d" % step, 0.6, kernel_args, shapes, [VMEM((EXT, NV, 128), F32)] * 4)


def run_pair(rnd, t, table, blocks, source, adjoint, ghost, arrivals):
    kernel_args = [table, ghost[-1], *blocks, *source, *adjoint, *ghost[:-1], *arrivals]
    shapes = [VMEM(STATE, F32)] * 2
    shapes += [VMEM(OWN, F32)] * 2 if t == 0 else [VMEM(MSGS, F32)]

    scratch = [VMEM((EXT + RL, NV, 128), F32), VMEM((EXT, NV, 128), F32)] + [VMEM((EXT + RL, NV, 128), F32)] * 3
    return call(partial(pair_kernel, rnd, t), "pair%d_%d" % (rnd, t), 1.8, kernel_args, shapes, scratch)


def ghost_send(part, table, blocks, source, adjoint):
    return call(partial(ghost_send_kernel, part), "ghost_send", 0.5,
                [table, blocks, source, adjoint], [VMEM(GHOST, F32)] * 2)


def ghost_receive(near, far):
    return call(ghost_receive_kernel, "ghost_receive", 0.5, [near, far],
                [VMEM(BLOCKS, BF16), VMEM(STATE, F32), SMEM_TABLE],
                [VMEM(TABLE, jnp.int32), pltpu.SemaphoreType.DMA])


def to_rows(rnd, levels, results, outs):
    outs = [] if outs is None else list(outs)
    place = len(results)
    return call(partial(rows_kernel, rnd, levels), "rows%d_%d" % (rnd, levels[0]), 0.6 * len(levels),
                [*results, *outs], [VMEM(OUT, F32)] * 2,
                [VMEM((B * NV // 128, 128, 128), BF16)],
                input_output_aliases={place: 0, place + 1: 1} if outs else {})


def after(values, done):
    return lax.optimization_barrier((values, done))[0]


def per_device(rhs, adjoint_owned, owner_of, columns, lower, dinv):
    cells = lax.axis_size("cell")
    sections = lax.axis_size("lvl")
    lower = jnp.transpose(lower, (0, 2, 1, 3))
    columns = jnp.transpose(columns, (2, 0, 1))
    blocks, source, adjoint = ([None] * LV for _ in range(3))
    sent, table = relay(adjoint_owned, columns, owner_of)
    relayed = lax.all_to_all(sent.reshape(1, cells, B * NV), "cell", split_axis=1, concat_axis=1, tiled=True)
    relayed = relayed.reshape(ROWS, B * NV // 128, 128)
    for part in range(LV):
        blocks[part], source[part] = prepare(part, *after((lower, dinv, rhs), sent))
    adjoint[0], = adjoint_state((0,), table, relayed)

    near_of = [i ^ 1 for i in range(cells)]
    far_of = [(i + 1 if i % 2 else i - 1) % cells for i in range(cells)]

    def exchange(near, far):
        far_in = lax.ppermute(far, "cell", list(enumerate(far_of)))
        near_in = lax.ppermute(near, "cell", list(enumerate(near_of)))
        return near_in, far_in

    def shift_handoff(x, by):
        moves = [(0, 1), (sections - 1, sections - 2)]
        pairs = [(a * cells + i, b * cells + (i + by) % cells) for a, b in moves for i in range(cells)]
        return lax.ppermute(x, ("lvl", "cell"), pairs)

    def handoff(msgs, rnd):
        partner = [1, 0, 3, 2] if rnd % 2 == 0 else [3, 2, 1, 0]
        pairs = [(s * cells + i, partner[s] * cells + i) for s in range(sections) for i in range(cells)]
        return lax.ppermute(msgs, ("lvl", "cell"), pairs)

    ghosts = {}
    own = near = far = outs = None
    for step in range(2 * LV):
        rnd, t = divmod(step, LV)
        result, *sent_out = run_step(step, table, blocks[t], source[t], adjoint[t], own, near, far)
        if step == 0:
            adjoint[1:] = adjoint_state((1, 2, 3), table, after(relayed, sent_out[-1]))
        if step in GHOST_STEPS:
            part = GHOST_STEPS[step]
            shared = after((blocks[part], source[part], adjoint[part]), sent_out[-1])
            ghosts[part] = ghost_receive(*exchange(*ghost_send(part, table, *shared)))
        if t < LV - 1:
            own = sent_out[0]
            near, far = exchange(*sent_out[1:])
        elif rnd == 0:
            own, to_left, to_right = sent_out
            own, near, far = shift_handoff(own, 0), shift_handoff(to_right, 1), shift_handoff(to_left, -1)
        results = [result] if t == 0 else [*results, result]
        if t == LV - 1:
            outs = to_rows(rnd, tuple(range(LV)), results, outs)
    msgs = sent_out[0]
    for rnd in range(LV // 2, sections):
        msgs = handoff(msgs, rnd - 1)
        own_near, own_far = msgs[0], msgs[1]
        for t in (0, 2):
            parts = (LV - 1 - t, LV - 2 - t)
            arrivals = (own_near, own_far, *exchange(own_near, own_far))
            picked = [[x[p] for p in parts] for x in (blocks, source, adjoint)]
            first, second, *sent_out = run_pair(rnd, t, table, *picked, ghosts[parts[0]], arrivals)
            if t == 0:
                own_near, own_far = sent_out
            outs = to_rows(rnd, (t, t + 1), (first, second), outs)
        msgs = sent_out[0]
    return outs


def solution(mesh):
    return jax.shard_map(
        per_device,
        mesh=mesh,
        in_specs=(
            P("lvl", "cell", None),
            P("lvl", "cell", None),
            P("lvl", "cell"),
            P("lvl", "cell", None),
            P("lvl", "cell", None, None),
            P("lvl", "cell", None),
        ),
        out_specs=(P("lvl", "cell", None), P("lvl", "cell", None)),
        check_vma=False,
    )
```

```python
from functools import partial

import jax
import jax.numpy as jnp
from jax import lax
from jax.experimental import pallas as pl
from jax.experimental.pallas import tpu as pltpu
from jax.sharding import PartitionSpec as P

B = 64
NV = 16
K = 3
W = 8
LV = 4
RL = 16
ROWS = LV * RL
EXT = RL + 2 * W
VMEM = pltpu.VMEM
SMEM = pltpu.SMEM
F32 = jnp.float32
BF16 = jnp.bfloat16
MIB = 1 << 20


def in_vmem(x):
    return pltpu.with_memory_space_constraint(x, VMEM)


def in_hbm(x):
    return pltpu.with_memory_space_constraint(x, pltpu.HBM)


def in_smem(x):
    return pltpu.with_memory_space_constraint(x, SMEM)


def split(x):
    hi = x.astype(BF16)
    lo = (x - hi.astype(F32)).astype(BF16)
    return hi, lo


def nn(a, b):
    return jnp.dot(a, b, preferred_element_type=F32)


def nt(a, b):
    return lax.dot_general(a, b, (((1,), (1,)), ((), ())), preferred_element_type=F32)


def low_half(shape):
    return lax.broadcasted_iota(jnp.int32, shape, len(shape) - 1) % 128 < B


def other_half(x):
    return pltpu.roll(x, B, axis=x.ndim - 1)


def spread_matrix():
    row = lax.broadcasted_iota(jnp.int32, (B * NV, 128), 0) // NV
    col = lax.broadcasted_iota(jnp.int32, (B * NV, 128), 1) % B
    return jnp.where(row == col, 1.0, 0.0).astype(BF16)


def own_lane(rows):
    lane = lax.broadcasted_iota(jnp.int32, (rows, 128), 1) % NV
    vec = lax.broadcasted_iota(jnp.int32, (rows, 128), 0) % NV
    return lane == vec


def state_of_rows(load, wide_hi, wide_lo):
    mask = own_lane(NV)

    def one(row, carry):
        block = load(row)
        for chunk in range(B * NV // 128):
            value = jnp.broadcast_to(block[chunk:chunk + 1], (NV, 128))
            hi, lo = split(jnp.where(mask, value, 0.0))
            place = (pl.ds(pl.multiple_of(row * NV, NV), NV), pl.ds(chunk * 128, 128))
            wide_hi[place] = hi
            wide_lo[place] = lo
        return carry

    lax.fori_loop(0, RL, one, 0, unroll=2)
    row = lax.broadcasted_iota(jnp.int32, (256, 128), 0) // NV
    col = lax.broadcasted_iota(jnp.int32, (256, 128), 1) % B

    def add(part, total):
        spread = jnp.where(row + part * (256 // NV) == col, 1.0, 0.0).astype(BF16)
        lanes = pl.ds(pl.multiple_of(part * 256, 256), 256)
        return total + nn(wide_hi[:, lanes], spread) + nn(wide_lo[:, lanes], spread)

    out = lax.fori_loop(0, B * NV // 256, add, jnp.zeros((RL * NV, 128), F32))
    return out.reshape(RL, NV, 128)


def storage_level(part):
    section = lax.axis_index("lvl")
    return jnp.where(section < LV // 2, part, LV - 1 - part)


def relay_kernel(owned_hbm, columns_hbm, owner_hbm, sent_hbm, s_ref,
                 table, turn, owned_ref, columns_ref, owner_ref, sent_rows, sems):
    arrivals = [
        pltpu.make_async_copy(owned_hbm, owned_ref, sems.at[0]),
        pltpu.make_async_copy(columns_hbm, columns_ref, sems.at[1]),
        pltpu.make_async_copy(owner_hbm, owner_ref, sems.at[2]),
    ]
    for copy in arrivals:
        copy.start()
    for copy in arrivals:
        copy.wait()
    for group in range(ROWS // 8):
        base = group % 2 * 8
        for chunk in range(B * NV // 128):
            turn[group, pl.ds(chunk * 8, 8), :] = owned_ref[group // 2, base:base + 8, chunk * 128:(chunk + 1) * 128]
        for row in range(8):
            sent_rows[group * 8 + row] = turn[group, pl.ds(row, B * NV // 128, stride=8), :]
    sent_copy = pltpu.make_async_copy(sent_rows, sent_hbm, sems.at[3])
    sent_copy.start()
    cells = lax.axis_size("cell")
    span = RL * cells
    local = lax.broadcasted_iota(jnp.int32, columns_ref.shape, 2)
    offset = columns_ref[...] - local - lax.axis_index("cell") * RL
    offset = jnp.where(offset > span // 2, offset - span, offset)
    offset = jnp.where(offset < -(span // 2), offset + span, offset)
    place = jnp.clip(offset + local + W, 0, EXT - 1)
    for k in range(K):
        table[pl.ds(k * LV, LV), pl.ds(0, RL)] = place[k]
    owner = owner_ref[...]
    owner_row = owner % span
    owner_local = owner // span % LV * RL + owner_row % RL
    table[pl.ds(K * LV, LV), pl.ds(0, RL)] = owner_local // cells * cells + owner_row // RL
    table_copy = pltpu.make_async_copy(table, s_ref, sems.at[4])
    table_copy.start()
    table_copy.wait()
    sent_copy.wait()


def blocks_kernel(part, lower_hbm, dinv_hbm, rhs_hbm, w_ref, r_ref,
                  low, din, tiles, both, sems, wide_hi, wide_lo, rhs_ref, lines):
    level = storage_level(part)
    rhs_copy = pltpu.make_async_copy(rhs_hbm.at[level], rhs_ref, sems.at[2])
    copies = (
        pltpu.make_async_copy(lower_hbm.at[level], low, sems.at[0]),
        pltpu.make_async_copy(dinv_hbm.at[level], din, sems.at[1]),
    )
    for copy in (rhs_copy, *copies):
        copy.start()
    rhs_copy.wait()

    for half in range(2):
        for chunk in range(B * NV // 128):
            lines[half, pl.ds(chunk * 8, 8), :] = rhs_ref[half * 8:half * 8 + 8, chunk * 128:(chunk + 1) * 128]

    def load_rhs(row):
        return lines[row // 8, pl.ds(row % 8, B * NV // 128, stride=8), :]

    r_ref[...] = state_of_rows(load_rhs, wide_hi, wide_lo)
    left = low_half((B // 2, 128))
    left_wide = low_half((B, 128))
    for copy in copies:
        copy.wait()
    def turn_half(half, carry):
        start = pl.multiple_of(half * 8, 8)
        for k in range(K + 1):
            for chunk in range(B * B // 128):
                lanes = pl.ds(chunk * 128, 128)
                value = low[k, pl.ds(start, 8), lanes] if k < K else din[pl.ds(start, 8), lanes]
                tiles[half, k, pl.ds(chunk * 8, 8), :] = value
        return carry

    lax.fori_loop(0, 2, turn_half, 0)

    def row_blocks(half, row, slot):
        piece = [tiles[half, k, pl.ds(row, B // 2, stride=8), :] for k in range(K + 1)]
        turned = [other_half(p) for p in piece]
        both[slot, 0, pl.ds(0, B // 2, stride=2), :] = jnp.where(left, piece[0], turned[1])
        both[slot, 0, pl.ds(1, B // 2, stride=2), :] = jnp.where(left, turned[0], piece[1])
        both[slot, 1, pl.ds(0, B // 2, stride=2), :] = jnp.where(left, piece[2], turned[3])
        both[slot, 1, pl.ds(1, B // 2, stride=2), :] = jnp.where(left, turned[2], piece[3])
        first_tile, second = both[slot, 0], both[slot, 1]
        diag = other_half(second)[:, :B]
        diag_hi, diag_lo = split(diag)
        right_hi, right_lo = split(jnp.concatenate([first_tile, second], axis=1))
        top = nn(jnp.concatenate([diag_hi, diag_lo], axis=0), right_hi)
        product = top[:B] + top[B:] + nn(diag_hi, right_lo)
        tail = jnp.where(left_wide, product[:, 128:], second)
        hi, lo = split(jnp.concatenate([product[:, :128], tail], axis=1))
        w_ref[half * 8 + row] = jnp.concatenate([hi, lo], axis=0)

    def four_rows(pair, carry):
        for row in range(4):
            row_blocks(pair // 2, pair % 2 * 4 + row, row)
        return carry

    lax.fori_loop(0, RL // 4, four_rows, 0)


def adjoint_kernel(parts, s_ref, relayed_ref, *refs):
    *outs, wide_hi, wide_lo = refs
    for part, a_ref in zip(parts, outs):
        level = storage_level(part)

        def load(row):
            return relayed_ref[s_ref[K * LV + level, row]]

        a_ref[...] = state_of_rows(load, wide_hi, wide_lo)


def pack(x):
    half = x.shape[0] // 2
    return jnp.where(low_half((half, NV, 128)), x[:half], x[half:])


def unpack(x):
    turned = other_half(x)
    left = low_half(x.shape)
    return jnp.concatenate([jnp.where(left, x, turned), jnp.where(left, turned, x)], axis=0)


def is_even():
    return lax.axis_index("cell") % 2 == 0


def by_side(near, far, do):
    even = is_even()
    pl.when(even)(lambda: do(far, near))
    pl.when(jnp.logical_not(even))(lambda: do(near, far))


def in_eights(count, do):
    for i in range(count // 8):
        for j in range(8):
            do(i, j)


def forward_row(block, source, places, lookup, ghost=False):
    half = low_half((NV, 128))
    last = jnp.zeros_like(source) if ghost else -source
    if places is None:
        lhs = jnp.concatenate([jnp.zeros_like(source), jnp.where(half, 0.0, last)], axis=1)
    else:
        x0, x1, x2 = [lookup[i] for i in places]
        lhs = jnp.concatenate([jnp.where(half, x0, x1), jnp.where(half, x2, last)], axis=1)
    hi, lo = split(lhs)
    out = nt(jnp.concatenate([hi, lo], axis=0), block)
    out = out[:NV] + out[NV:]
    out = out + other_half(out)
    return source - out if ghost else -out


def clear(accs, window):
    for acc in accs:
        acc[pl.ds(0, window)] = jnp.zeros((window, NV, 128), F32)


def backward_row(block, value, places, accs):
    hi, lo = split(value)
    out = nn(jnp.concatenate([hi, lo], axis=0), block)
    out = out[:NV] + out[NV:]
    accs[0][places[0]] += out[:, :128]
    accs[1][places[1]] += out[:, :128]
    accs[2][places[2]] += out[:, 128:]
    return out[:, 128:]


def collected(accs, window):
    acc0, acc1, acc2 = [acc[pl.ds(0, window)] for acc in accs]
    total = jnp.where(low_half((window, NV, 128)), acc0 + acc2, acc1)
    return total + other_half(total)


def step_kernel(step, s_ref, w_ref, r_ref, a_ref, own_ref, near_ref, far_ref, res_ref, *refs):
    *outs, ext, acc0, acc1, acc2 = refs
    section = lax.axis_index("lvl")
    rnd, t = divmod(step, LV)
    first, handed = step == 0, t == 0

    def incoming(do):
        if handed:
            do(near_ref, far_ref)
        else:
            by_side(near_ref, far_ref, do)

    def outgoing(to_left, to_right, own):
        def put(near, far):
            if len(outs) == 1:
                outs[0][0] = near
                outs[0][1] = far
            else:
                outs[1][...] = near
                outs[2][...] = far

        if len(outs) == 3:
            outs[0][...] = own
        if len(outs) == 3 and t == LV - 1:
            put(to_left, to_right)
        else:
            even = is_even()
            pl.when(even)(lambda: put(to_right, to_left))
            pl.when(jnp.logical_not(even))(lambda: put(to_left, to_right))

    @pl.when(section == rnd)
    def _():
        if not first:
            ext[pl.ds(W, RL)] = unpack(own_ref[...])

            def fill(from_left, from_right):
                ext[pl.ds(0, W)] = unpack(from_left[...])
                ext[pl.ds(W + RL, W)] = unpack(from_right[...])

            incoming(fill)

        def one(i, j):
            q = i * 8 + j
            places = None if first else [s_ref[k * LV + t, q] for k in range(K)]
            res_ref[q] = forward_row(w_ref[q], r_ref[q], places, ext)

        in_eights(RL, one)
        x = res_ref[...]
        if len(outs) == 1:
            outgoing(pack(x), pack(x), None)
        else:
            outgoing(pack(x[:W]), pack(x[W:]), pack(x))

    @pl.when(section == LV - 1 - rnd)
    def _():
        level = LV - 1 - t
        if not first:
            ext[pl.ds(0, RL)] = unpack(own_ref[...])

            def add(from_left, from_right):
                ext[pl.ds(0, W)] += unpack(from_left[...])
                ext[pl.ds(W, W)] += unpack(from_right[...])

            incoming(add)
        accs = (acc0, acc1, acc2)
        clear(accs, EXT)

        def one(i, j):
            q = i * 8 + j
            value = a_ref[q] if first else a_ref[q] - ext[q]
            res_ref[q] = backward_row(w_ref[q], value, [s_ref[k * LV + level, q] for k in range(K)], accs)

        in_eights(RL, one)
        total = collected(accs, EXT)
        if len(outs) == 1:
            outgoing(pack(total[:RL]), pack(total[RL:]), None)
        else:
            outgoing(pack(total[:W]), pack(total[W + RL:]), pack(total[W:W + RL]))


def pair_kernel(rnd, t, s_ref, ghost_s, w0_ref, w1_ref, r0_ref, r1_ref, a0_ref, a1_ref, g_ref, gs_ref,
                own_near, own_far, near_ref, far_ref, res0_ref, res1_ref, *refs):
    *outs, ext, ext2, acc0, acc1, acc2 = refs
    section = lax.axis_index("lvl")

    def outgoing(to_left, to_right):
        def put(near, far):
            if len(outs) == 1:
                outs[0][0] = near
                outs[0][1] = far
            else:
                outs[0][...] = near
                outs[1][...] = far

        even = is_even()
        pl.when(even)(lambda: put(to_right, to_left))
        pl.when(jnp.logical_not(even))(lambda: put(to_left, to_right))

    def own_places(level, q, shift):
        return [s_ref[k * LV + level, q] + shift for k in range(K)]

    def ghost_places(ghost):
        return [ghost_s[k, ghost] for k in range(K)]

    @pl.when(section == rnd)
    def _():
        ext[pl.ds(RL, RL)] = unpack(own_near[...])

        def fill(from_left, from_right):
            ext[pl.ds(0, RL)] = unpack(from_left[...])
            ext[pl.ds(2 * RL, RL)] = unpack(from_right[...])

        by_side(near_ref, far_ref, fill)

        def ghost_row(i, j):
            ghost = i * 8 + j
            ext2[i * (W + RL) + j] = forward_row(g_ref[ghost], gs_ref[ghost], ghost_places(ghost), ext, True)

        def first_row(i, j):
            q = i * 8 + j
            x = forward_row(w0_ref[q], r0_ref[q], own_places(t, q, W), ext)
            ext2[W + q] = x
            res0_ref[q] = x

        def second_row(i, j):
            q = i * 8 + j
            res1_ref[q] = forward_row(w1_ref[q], r1_ref[q], own_places(t + 1, q, 0), ext2)

        in_eights(2 * W, ghost_row)
        in_eights(RL, first_row)
        in_eights(RL, second_row)
        x = res1_ref[...]
        outgoing(pack(x), pack(x))

    @pl.when(section == LV - 1 - rnd)
    def _():
        level = LV - 1 - t

        def gather(own_left, own_right):
            ext[pl.ds(0, RL)] = unpack(own_left[...])
            ext[pl.ds(RL, RL)] = unpack(own_right[...])

        def add(from_left, from_right):
            ext[pl.ds(0, RL)] += unpack(from_left[...])
            ext[pl.ds(RL, RL)] += unpack(from_right[...])

        by_side(own_near, own_far, gather)
        by_side(near_ref, far_ref, add)
        accs = (acc0, acc1, acc2)
        clear(accs, EXT + RL)

        def ghost_row(i, j):
            ghost = i * 8 + j
            backward_row(g_ref[ghost], gs_ref[ghost] - ext[i * (W + RL) + j], ghost_places(ghost), accs)

        def first_row(i, j):
            q = i * 8 + j
            res0_ref[q] = backward_row(w0_ref[q], a0_ref[q] - ext[W + q], own_places(level, q, W), accs)

        in_eights(2 * W, ghost_row)
        in_eights(RL, first_row)
        ext2[pl.ds(0, RL)] = collected(accs, EXT + RL)[RL:2 * RL]
        clear(accs, EXT)

        def second_row(i, j):
            q = i * 8 + j
            res1_ref[q] = backward_row(w1_ref[q], a1_ref[q] - ext2[q], own_places(level - 1, q, 0), accs)

        in_eights(RL, second_row)
        total = collected(accs, EXT)
        outgoing(pack(total[:RL]), pack(total[RL:]))


def ghost_send_kernel(part, s_ref, w_ref, r_ref, a_ref, near_ref, far_ref):
    forward = lax.axis_index("lvl") >= LV // 2
    shift = jnp.where(is_even(), W, 0)
    sub = lax.broadcasted_iota(jnp.int32, (8, 128), 0)
    left = low_half((B // 2, 128))
    left8 = low_half((8, 128))
    level = storage_level(part)
    for out_ref, base in ((near_ref, shift), (far_ref, W - shift)):

        def one(i, carry):
            block = w_ref[base + i]
            block = block[:B].astype(F32) + block[B:].astype(F32)
            out_ref[i, pl.ds(0, B), :] = block[:, :128]
            third = block[:, 128:]
            out_ref[i, pl.ds(B, B // 2), :] = jnp.where(left, third[:B // 2], other_half(third[B // 2:]))
            direct = forward_row(w_ref[base + i], r_ref[base + i], None, None)
            value = jnp.where(forward, direct, a_ref[base + i])
            out_ref[i, pl.ds(96, 8), :] = jnp.where(left8, value[:8], value[8:])
            places = jnp.zeros((8, 128), F32)
            for k in range(K):
                place = s_ref[k * LV + level, base + i].astype(F32)
                places = jnp.where(sub == k, place, places)
            out_ref[i, pl.ds(104, 8), :] = places
            return carry

        lax.fori_loop(0, W, one, 0)


def ghost_receive_kernel(near_ref, far_ref, g_ref, gs_ref, t_ref, table, sem):
    shift = jnp.where(is_even(), W, 0)
    lane = lax.broadcasted_iota(jnp.int32, (8, 128), 1)
    left = low_half((B // 2, 128))
    places = jnp.zeros((8, 128), F32)
    for in_ref, base in ((near_ref, shift), (far_ref, W - shift)):

        def one(i, places):
            first = in_ref[i, pl.ds(0, B), :]
            packed = in_ref[i, pl.ds(B, B // 2), :]
            third = jnp.concatenate(
                [jnp.where(left, packed, 0.0), jnp.where(left, other_half(packed), 0.0)], axis=0)
            hi, lo = split(jnp.concatenate([first, third], axis=1))
            g_ref[base + i] = jnp.concatenate([hi, lo], axis=0)
            gs_ref[base + i] = unpack(in_ref[i, pl.ds(96, 8), :].reshape(1, 8, 128)).reshape(NV, 128)
            return jnp.where(lane == base + i, in_ref[i, pl.ds(104, 8), :], places)

        places = lax.fori_loop(0, W, one, places)
    places = places.astype(jnp.int32) + jnp.where(lane < W, -W, RL + W)
    table[pl.ds(0, 8), :] = jnp.clip(places, 0, EXT + RL - 1)
    table[pl.ds(8, 8), :] = jnp.zeros((8, 128), jnp.int32)
    copy = pltpu.make_async_copy(table, t_ref, sem)
    copy.start()
    copy.wait()


def rows_kernel(rnd, levels, *refs):
    *refs, sol_ref, adj_ref, spread_ref, lines = refs
    results = refs[:len(levels)]
    section = lax.axis_index("lvl")
    forward = section == rnd

    @pl.when(jnp.logical_or(forward, section == LV - 1 - rnd))
    def _():
        spread = jnp.where(low_half((B * NV, 128)), 0.0, spread_matrix().astype(F32)).astype(BF16)
        spread_ref[...] = spread.reshape(B * NV // 128, 128, 128)
        mask = own_lane(RL * NV)
        for t, x in zip(levels, results):
            hi, lo = split(x[...].reshape(RL * NV, 128))

            def one(chunk, carry):
                part = spread_ref[chunk]
                wide = jnp.where(mask, nt(hi, part) + nt(lo, part), 0.0)
                lines[chunk] = jnp.sum(wide.reshape(RL, NV, 128), axis=1)
                return carry

            lax.fori_loop(0, B * NV // 128, one, 0, unroll=8 if rnd == LV - 1 and levels[0] else 2)
            for chunk in range(B * NV // 128):
                lanes = pl.ds(chunk * 128, 128)

                @pl.when(forward)
                def _():
                    sol_ref[t, :, lanes] = lines[chunk]

                @pl.when(jnp.logical_not(forward))
                def _():
                    adj_ref[LV - 1 - t, :, lanes] = lines[chunk]


def vspec():
    return pl.BlockSpec(memory_space=VMEM)


def sspec():
    return pl.BlockSpec(memory_space=SMEM)


def hspec():
    return pl.BlockSpec(memory_space=pl.ANY)


STATE = (RL, NV, 128)
OWN = (RL // 2, NV, 128)
SIDE = (W // 2, NV, 128)
MSGS = (2, RL // 2, NV, 128)
GHOST = (W, 112, 128)
GHOST_STEPS = {1: 3, 2: 1}
TABLE = ((K + 1) * LV, 128)
BLOCKS = (RL, 2 * B, 256)
SMEM_TABLE = SMEM(TABLE, jnp.int32)
OUT = (LV, RL, B * NV)


def params(mib):
    return pltpu.CompilerParams(vmem_limit_bytes=mib * MIB)


def cost(us):
    return pl.CostEstimate(flops=int(us * 1e9), bytes_accessed=int(us * 3e6), transcendentals=0)


def relay(owned, columns, owner):
    sent = (ROWS, B * NV // 128, 128)
    return pl.pallas_call(
        relay_kernel,
        out_shape=(pltpu.HBM(sent, F32), SMEM_TABLE),
        in_specs=[hspec()] * 3,
        out_specs=(hspec(), sspec()),
        scratch_shapes=[
            VMEM(TABLE, jnp.int32),
            VMEM((ROWS // 8, B * NV // 16, 128), F32),
            VMEM(owned.shape, F32),
            VMEM(columns.shape, jnp.int32),
            VMEM(owner.shape, jnp.int32),
            VMEM(sent, F32),
            pltpu.SemaphoreType.DMA((5,)),
        ],
        compiler_params=params(8),
        cost_estimate=cost(2.0),
        name="relay",
    )(in_hbm(owned), in_hbm(columns), in_hbm(owner))


def prepare(part, lower, dinv, rhs):
    wide = VMEM((RL * NV, B * NV), BF16)
    scratch = [
        VMEM((K, RL, B * B), F32),
        VMEM((RL, B * B), F32),
        VMEM((2, K + 1, 8 * B * B // 128, 128), F32),
        VMEM((4, 2, B, 128), F32),
        pltpu.SemaphoreType.DMA((3,)),
        wide,
        wide,
        VMEM((RL, B * NV), F32),
        VMEM((2, B * NV // 16, 128), F32),
    ]
    shapes = [VMEM(BLOCKS, BF16), VMEM(STATE, F32)]
    specs = [hspec(), hspec(), hspec()]
    return pl.pallas_call(
        partial(blocks_kernel, part),
        out_shape=shapes,
        in_specs=specs,
        out_specs=[vspec()] * len(shapes),
        scratch_shapes=scratch,
        compiler_params=params(12),
        cost_estimate=cost(2.5),
        name="prepare%d" % part,
    )(in_hbm(lower), in_hbm(dinv), in_hbm(rhs))


def adjoint_state(parts, table, relayed):
    wide = VMEM((RL * NV, B * NV), BF16)
    return call(partial(adjoint_kernel, parts), "adjoint_state", 0.6 * len(parts), [table, relayed],
                [VMEM(STATE, F32)] * len(parts), [wide, wide])


def call(body, name, us, kernel_args, shapes, scratch=(), mib=8, **more):
    def place(x):
        return in_smem(x) if x.dtype == jnp.int32 and x.shape == TABLE else in_vmem(x)

    def spec(x):
        return sspec() if x.dtype == jnp.int32 and x.shape == TABLE else vspec()

    return pl.pallas_call(
        body,
        out_shape=tuple(shapes),
        in_specs=[spec(x) for x in kernel_args],
        out_specs=tuple(sspec() if isinstance(x, type(SMEM_TABLE)) and x.memory_space == SMEM else vspec() for x in shapes),
        scratch_shapes=list(scratch),
        compiler_params=params(mib),
        cost_estimate=cost(us),
        name=name,
        **more,
    )(*[place(x) for x in kernel_args])


def run_step(step, table, blocks, source, adjoint, own, near, far):
    kernel_args = [table, blocks, source, adjoint]
    if own is not None:
        kernel_args += [own, near, far]

    def body(*refs):
        head, refs = refs[:4], refs[4:]
        arrivals = [None] * 3
        if own is not None:
            arrivals, refs = refs[:3], refs[3:]
        step_kernel(step, *head, *arrivals, *refs)

    shapes = [VMEM(STATE, F32)]
    shapes += [VMEM(MSGS, F32)] if step == 2 * LV - 1 else [VMEM(OWN, F32), VMEM(SIDE, F32), VMEM(SIDE, F32)]
    return call(body, "step%d" % step, 0.6, kernel_args, shapes, [VMEM((EXT, NV, 128), F32)] * 4)


def run_pair(rnd, t, table, blocks, source, adjoint, ghost, arrivals):
    kernel_args = [table, ghost[-1], *blocks, *source, *adjoint, *ghost[:-1], *arrivals]
    shapes = [VMEM(STATE, F32)] * 2
    shapes += [VMEM(OWN, F32)] * 2 if t == 0 else [VMEM(MSGS, F32)]

    scratch = [VMEM((EXT + RL, NV, 128), F32), VMEM((EXT, NV, 128), F32)] + [VMEM((EXT + RL, NV, 128), F32)] * 3
    return call(partial(pair_kernel, rnd, t), "pair%d_%d" % (rnd, t), 1.8, kernel_args, shapes, scratch)


def ghost_send(part, table, blocks, source, adjoint):
    return call(partial(ghost_send_kernel, part), "ghost_send", 0.5,
                [table, blocks, source, adjoint], [VMEM(GHOST, F32)] * 2)


def ghost_receive(near, far):
    return call(ghost_receive_kernel, "ghost_receive", 0.5, [near, far],
                [VMEM(BLOCKS, BF16), VMEM(STATE, F32), SMEM_TABLE],
                [VMEM(TABLE, jnp.int32), pltpu.SemaphoreType.DMA])


def to_rows(rnd, levels, results, outs):
    outs = [] if outs is None else list(outs)
    place = len(results)
    return call(partial(rows_kernel, rnd, levels), "rows%d_%d" % (rnd, levels[0]), 0.6 * len(levels),
                [*results, *outs], [VMEM(OUT, F32)] * 2,
                [VMEM((B * NV // 128, 128, 128), BF16), VMEM((B * NV // 128, RL, 128), F32)],
                input_output_aliases={place: 0, place + 1: 1} if outs else {})


def after(values, done):
    return lax.optimization_barrier((values, done))[0]


def per_device(rhs, adjoint_owned, owner_of, columns, lower, dinv):
    cells = lax.axis_size("cell")
    sections = lax.axis_size("lvl")
    lower = jnp.transpose(lower, (0, 2, 1, 3))
    columns = jnp.transpose(columns, (2, 0, 1))
    blocks, source, adjoint = ([None] * LV for _ in range(3))
    sent, table = relay(adjoint_owned, columns, owner_of)
    relayed = lax.all_to_all(sent.reshape(1, cells, B * NV), "cell", split_axis=1, concat_axis=1, tiled=True)
    relayed = relayed.reshape(ROWS, B * NV // 128, 128)
    for part in range(LV):
        blocks[part], source[part] = prepare(part, *after((lower, dinv, rhs), sent))
    adjoint[0], = adjoint_state((0,), table, relayed)

    near_of = [i ^ 1 for i in range(cells)]
    far_of = [(i + 1 if i % 2 else i - 1) % cells for i in range(cells)]

    def exchange(near, far):
        far_in = lax.ppermute(far, "cell", list(enumerate(far_of)))
        near_in = lax.ppermute(near, "cell", list(enumerate(near_of)))
        return near_in, far_in

    def shift_handoff(x, by):
        moves = [(0, 1), (sections - 1, sections - 2)]
        pairs = [(a * cells + i, b * cells + (i + by) % cells) for a, b in moves for i in range(cells)]
        return lax.ppermute(x, ("lvl", "cell"), pairs)

    def handoff(msgs, rnd):
        partner = [1, 0, 3, 2] if rnd % 2 == 0 else [3, 2, 1, 0]
        pairs = [(s * cells + i, partner[s] * cells + i) for s in range(sections) for i in range(cells)]
        return lax.ppermute(msgs, ("lvl", "cell"), pairs)

    ghosts = {}
    own = near = far = outs = None
    for step in range(2 * LV):
        rnd, t = divmod(step, LV)
        result, *sent_out = run_step(step, table, blocks[t], source[t], adjoint[t], own, near, far)
        if step == 0:
            adjoint[1:] = adjoint_state((1, 2, 3), table, after(relayed, sent_out[-1]))
        if step in GHOST_STEPS:
            part = GHOST_STEPS[step]
            shared = after((blocks[part], source[part], adjoint[part]), sent_out[-1])
            ghosts[part] = ghost_receive(*exchange(*ghost_send(part, table, *shared)))
        if t < LV - 1:
            own = sent_out[0]
            near, far = exchange(*sent_out[1:])
        elif rnd == 0:
            own, to_left, to_right = sent_out
            own, near, far = shift_handoff(own, 0), shift_handoff(to_right, 1), shift_handoff(to_left, -1)
        results = [result] if t == 0 else [*results, result]
        if t == LV - 1:
            outs = to_rows(rnd, tuple(range(LV)), results, outs)
    msgs = sent_out[0]
    for rnd in range(LV // 2, sections):
        msgs = handoff(msgs, rnd - 1)
        own_near, own_far = msgs[0], msgs[1]
        for t in (0, 2):
            parts = (LV - 1 - t, LV - 2 - t)
            arrivals = (own_near, own_far, *exchange(own_near, own_far))
            picked = [[x[p] for p in parts] for x in (blocks, source, adjoint)]
            first, second, *sent_out = run_pair(rnd, t, table, *picked, ghosts[parts[0]], arrivals)
            if t == 0:
                own_near, own_far = sent_out
            outs = to_rows(rnd, (t, t + 1), (first, second), outs)
        msgs = sent_out[0]
    return outs


def solution(mesh):
    return jax.shard_map(
        per_device,
        mesh=mesh,
        in_specs=(
            P("lvl", "cell", None),
            P("lvl", "cell", None),
            P("lvl", "cell"),
            P("lvl", "cell", None),
            P("lvl", "cell", None, None),
            P("lvl", "cell", None),
        ),
        out_specs=(P("lvl", "cell", None), P("lvl", "cell", None)),
        check_vma=False,
    )
```
